32 devices in a mesh: groups: 2 (over y), gz: 4 (over z), gy: 2 (over x), col: 2 (over core).
Axes of the slice: x: 2, y: 2, z: 4, core: 2. Of those that a mesh axis runs over, the one named last changes fastest.
Arguments:
- fields: float32 [4, 6, 32, 32, 256], P('groups', None, ('gz', 'col'), 'gy'), parts along dimension 0, may hold values from -6 to 6
- eps_inv: float32 [64, 32, 256], P(('groups', 'gz', 'col'), 'gy'), parts along dimension 0, may hold values from 0.0826 to 1
- row_counts: int32 [4, 8], P(('groups', 'gy')), parts along dimension 0, may hold values from 1 to 4, 16 in all within a row
- col_counts: int32 [256], P('groups'), parts along dimension 0, may hold values from 1 to 4, 256 in all
- density: float32 [32, 128], P(('groups', 'gy')), parts along dimension 0, may hold values from 0 to 1
Outputs:
- fields_out: float32 [4, 6, 32, 32, 256], P('groups', None, ('gz', 'col'), 'gy'), parts along dimension 0
- design_gradient: float32 [32, 128], P(('groups', 'gy'), ('gz', 'col')), parts along dimension 0
The draws below stay inside these ranges and needn't reach their ends.
There are 2 independent parts, one for each index of `groups`. The reference program is written for one: setup_inputs(seed, part) draws one part's arguments, and reference() takes and returns one part's arrays. A program takes and returns all parts, laid end to end along the dimension named above; each array names one. Nothing has to cross between parts.
Inputs may be any that keep to these rules, and one draw needn't show every extreme that they name: `row_counts`: each row of 8 counts sums to 16, so a y-block of the field maps onto the design rows of that block. `col_counts`: the 128 counts sum to 256.
All inputs are finite; a program needn't handle non-finite values.
Results may differ from the reference program's by a relative error of at most 0.0003.
Values sent between devices are 32-bit elements; how exact they have to be, the bound alone decides.
No kernel may reach another device: no remote copies, remote signals or barrier semaphores. Data moves between devices by JAX's collectives and lax.ppermute only.
A program may use at most 64 MiB of HBM per device.

```python
import math
import jax
import jax.numpy as jnp
import numpy as np
from jax import lax

CY = 16
CX = 256
STEPS = 8
ROW_MOST = 4
COL_MOST = 4
FILTER_LEN = 12
NZ = 32
NY = 32
NX = 256
DBAND = 8
MY = 16
MX = 128
LAYER_START = 10
LAYER_DEPTH = 12
N_GY = 2


def levels(rng, shape, pieces, low, largest):
    gain, own = 1.0, jax.random.fold_in(rng, 6)
    for axis_at, shards_of in pieces:
        steps = jnp.exp(jax.random.uniform(jax.random.fold_in(own, axis_at), (shards_of,), jnp.float32, low / len(pieces), largest / len(pieces)))
        gain = gain * jnp.repeat(steps, shape[axis_at] // shards_of).reshape([-1 if axis == axis_at else 1 for axis in range(len(shape))])
    return gain


def profile(number_of, total, reach, skew):
    loads = [(1 << 20) // math.isqrt(rank ** skew) + 1 for rank in range(2, number_of + 1)]
    surplus, holding = total - reach - (number_of - 1), [1] * (number_of - 1)
    while surplus > 0:
        movable = [i for i in range(number_of - 1) if holding[i] < reach]
        pool, remaining = sum([loads[i] for i in movable]), surplus
        for i in movable:
            extra = min(reach - holding[i], max(1, remaining * loads[i] // pool), surplus)
            holding[i] = holding[i] + extra
            surplus = surplus - extra
    return np.array([reach] + holding)


def ragged(stream_key, count, total, most, lean):
    if count == 2:
        one = jax.random.randint(stream_key, (), max(1, total - most), min(most, total - 1) + 1)
        return jnp.stack([one, total - one])
    tallies = jnp.asarray(profile(count, total, most, lean), jnp.int32)
    pairs = (count - 1) // 2
    giver, taker = tallies[1:1 + 2 * pairs:2], tallies[2:2 + 2 * pairs:2]
    slack = jnp.minimum(giver - 1, most - taker)
    moved = jax.random.randint(jax.random.fold_in(stream_key, 1), (pairs,), 0, 1 << 20) % (slack + 1)
    tallies = tallies.at[1:1 + 2 * pairs:2].set(giver - moved).at[2:2 + 2 * pairs:2].set(taker + moved)
    return tallies[jax.random.permutation(jax.random.fold_in(stream_key, 2), count)]


def bell_draw(rng, dims, scale, bound, cuts=(), kind=jnp.bfloat16):
    gain = levels(rng, dims, cuts, -0.22, 0.18) if cuts else 1.0
    array = jax.random.normal(rng, dims, jnp.float32) * scale * gain
    return jnp.minimum(jnp.maximum(array, -bound), bound).astype(kind)


def setup_inputs(seed: int = 0, part: int = 0) -> dict:
    key_of = jax.random.split(jax.random.key(seed), 6)
    own_keys = jax.random.split(jax.random.fold_in(key_of[5], part), 6)
    return {
        "fields": bell_draw(own_keys[0], (2, 6, NZ, NY, NX), 1.0, 6.0, ((2, 8), (3, 2)), jnp.float32),
        "eps_inv": jnp.clip(jnp.exp(math.log(1.0) - 2.4937456 * jax.random.uniform(own_keys[1], (NZ, NY, NX), jnp.float32) ** levels(own_keys[1], (NZ, NY, NX), ((0, 8), (1, 2)), -0.2, 0.2)), 0.0826, 1.0),
        "row_counts": jax.vmap(lambda own: ragged(own, DBAND, CY, ROW_MOST, 1))(jax.random.split(own_keys[2], N_GY)).reshape((N_GY, DBAND)).astype(jnp.int32),
        "col_counts": ragged(own_keys[3], MX, CX, COL_MOST, 1).astype(jnp.int32),
        "density": jnp.clip(1.0 * jax.random.uniform(own_keys[4], (MY, MX), jnp.float32) ** levels(own_keys[4], (MY, MX), ((0, 2),), -0.2, 0.2), 0.0, 1.0),
    }


courant = 0.5
omega_step = 0.7
beta_proj = 4.0
eta_proj = 0.5
eps_span = 11.1


def shifted_ahead(field, axis):
    size = field.shape[axis]
    tail = jnp.zeros_like(lax.slice_in_dim(field, 0, 1, axis=axis))
    return jnp.concatenate([lax.slice_in_dim(field, 1, size, axis=axis), tail], axis=axis) - field


def shifted_behind(field, axis):
    size = field.shape[axis]
    head = jnp.zeros_like(lax.slice_in_dim(field, 0, 1, axis=axis))
    return field - jnp.concatenate([head, lax.slice_in_dim(field, 0, size - 1, axis=axis)], axis=axis)


def yee_step(state, scale):
    ex, ey, ez, hx, hy, hz = state
    hx = hx - courant * (shifted_ahead(ez, 2) - shifted_ahead(ey, 1))
    hy = hy - courant * (shifted_ahead(ex, 1) - shifted_ahead(ez, 3))
    hz = hz - courant * (shifted_ahead(ey, 3) - shifted_ahead(ex, 2))
    ex = ex + scale * (shifted_behind(hz, 2) - shifted_behind(hy, 1))
    ey = ey + scale * (shifted_behind(hx, 1) - shifted_behind(hz, 3))
    ez = ez + scale * (shifted_behind(hy, 3) - shifted_behind(hx, 2))
    return (ex, ey, ez, hx, hy, hz)


def slope_of(density):
    norm = math.tanh(beta_proj * eta_proj) + math.tanh(beta_proj * (1.0 - eta_proj))
    bent = jnp.tanh(beta_proj * (density - eta_proj))
    return beta_proj * (1.0 - bent * bent) / norm


def band_table(counts, length):
    ends = jnp.cumsum(counts).astype(jnp.int32)
    starts = ends - counts
    place = jnp.arange(length, dtype=jnp.int32)[:, None]
    return ((place >= starts[None, :]) & (place < ends[None, :])).astype(jnp.float32)


def reference(fields, eps_inv, row_counts, col_counts, density):
    scale = courant * eps_inv
    state = tuple(fields[:, c] for c in range(6))
    acc_re = jnp.zeros((2, 3) + eps_inv.shape, jnp.float32)
    acc_im = jnp.zeros((2, 3) + eps_inv.shape, jnp.float32)
    for step in range(STEPS):
        state = yee_step(state, scale)
        angle = omega_step * (step + 1)
        electric = jnp.stack(state[:3], axis=1)
        acc_re = acc_re + electric * math.cos(angle)
        acc_im = acc_im - electric * math.sin(angle)
    fields_out = jnp.stack(state, axis=1)
    product = jnp.sum(acc_re[0] * acc_re[1] - acc_im[0] * acc_im[1], axis=0)
    column_sum = jnp.sum(product[LAYER_START:LAYER_START + LAYER_DEPTH], axis=0)
    rows = band_table(row_counts.reshape(-1).astype(jnp.int32), NY)
    cols = band_table(col_counts.astype(jnp.int32), NX)
    inner = jnp.dot(column_sum, cols, precision=lax.Precision.HIGHEST, preferred_element_type=jnp.float32)
    sens = jnp.dot(rows.T, inner, precision=lax.Precision.HIGHEST, preferred_element_type=jnp.float32)
    sens = sens * (eps_span / (STEPS * LAYER_DEPTH))
    weighted = sens * slope_of(density)
    wave_y = jnp.sin(math.pi * jnp.arange(MY, dtype=jnp.float32) / MY)
    wave_x = jnp.sin(math.pi * jnp.arange(MX, dtype=jnp.float32) / MX)
    response = 1.0 / (1.0 + FILTER_LEN ** 2 * (4.0 * wave_y[:, None] ** 2 + 4.0 * wave_x[None, :] ** 2))
    filtered = jnp.real(jnp.fft.ifft2(jnp.fft.fft2(weighted) * response))
    return fields_out, filtered.astype(jnp.float32)
```

```python
import functools
import math

import jax
import jax.numpy as jnp
import numpy as np
from jax import lax
from jax.experimental import pallas as pl
from jax.experimental.pallas import tpu as pltpu
from jax.sharding import PartitionSpec as P

STEPS = 8
FILTER_LEN = 12

courant = 0.5
omega_step = 0.7
beta_proj = 4.0
eta_proj = 0.5
eps_span = 11.1
highest = lax.Precision.HIGHEST

PLANES = 13
Z = ("gz", "col")


def slope_of(density):
    norm = math.tanh(beta_proj * eta_proj) + math.tanh(beta_proj * (1.0 - eta_proj))
    bent = jnp.tanh(beta_proj * (density - eta_proj))
    return beta_proj * (1.0 - bent * bent) / norm


def real_basis(size):
    place = np.arange(size)
    rows, waves = [], []
    for k in range(size // 2 + 1):
        angle = 2.0 * np.pi * ((k * place) % size) / size
        edge = k == 0 or 2 * k == size
        rows.append(np.cos(angle) * math.sqrt((1.0 if edge else 2.0) / size))
        waves.append(k)
        if not edge:
            rows.append(np.sin(angle) * math.sqrt(2.0 / size))
            waves.append(k)
    return np.array(rows), np.array(waves)


def band_table(counts, place):
    ends = jnp.cumsum(counts)
    starts = ends - counts
    return ((place >= starts[None, :]) & (place < ends[None, :])).astype(jnp.float32)


def mm(left, right):
    return jnp.dot(left, right, precision=highest, preferred_element_type=jnp.float32)


def window_kernel(cfg, *refs):
    depth, rows_own, rows, sides, masked_rows = cfg
    n_blocks = 5
    it = iter(refs)
    info = next(it)
    full = [next(it) for _ in range(n_blocks)]
    halo = [[next(it) for _ in range(n_blocks)] for _ in range(sides)]
    row_table, col_table, slope, basis_x, basis_xt, basis_y, own_y, response = (next(it) for _ in range(8))
    out, share = next(it), next(it)
    st, acc, sem_full, sem_halo, sem_out = (next(it) for _ in range(5))

    halo_rows = STEPS
    core = info[0]
    row_own = pl.multiple_of(info[1], 8)
    copies = []
    for b in range(n_blocks):
        place = jnp.where(core == 0, b * depth, (n_blocks - 1 - b) * depth)
        layers = pl.ds(place, depth)
        copies.append(
            pltpu.make_async_copy(full[b], st.at[:, layers, pl.ds(row_own, rows_own), :], sem_full.at[b])
        )
        for s in range(sides):
            row_at = pl.multiple_of(info[2 + s], 8)
            copies.append(
                pltpu.make_async_copy(
                    halo[s][b], st.at[:, layers, pl.ds(row_at, halo_rows), :], sem_halo.at[s, b]
                )
            )
    for copy in copies:
        copy.start()
    acc[...] = jnp.zeros_like(acc)
    for copy in copies:
        copy.wait()

    nx = st.shape[-1]
    row_at = lax.broadcasted_iota(jnp.int32, (rows, nx), 0)
    lane_at = lax.broadcasted_iota(jnp.int32, (rows, nx), 1)
    last_row, first_row = row_at == rows - 1, row_at == 0
    last_lane, first_lane = lane_at == nx - 1, lane_at == 0
    if masked_rows:
        row_ok = (row_at >= info[6]) & (row_at < info[7])

    def y_ahead(f):
        return jnp.where(last_row, 0.0, pltpu.roll(f, rows - 1, 0))

    def y_behind(f):
        return jnp.where(first_row, 0.0, pltpu.roll(f, 1, 0))

    def x_ahead(f):
        return jnp.where(last_lane, 0.0, pltpu.roll(f, nx - 1, 1))

    def x_behind(f):
        return jnp.where(first_lane, 0.0, pltpu.roll(f, 1, 1))

    low_layer, high_layer = info[4], info[5]

    def layer(z, carry, weights):
        coef = jnp.where((z >= low_layer) & (z < high_layer), courant, 0.0)
        coef = jnp.full((rows, nx), coef, jnp.float32)
        if masked_rows:
            coef = jnp.where(row_ok, coef, 0.0)
        scale = st[12, z]
        carried = []
        for r in range(2):
            hx_p, hy_p = carry[r]
            b = 6 * r
            ex, ey, ez = st[b, z], st[b + 1, z], st[b + 2, z]
            ex_n, ey_n = st[b, z + 1], st[b + 1, z + 1]
            hx = st[b + 3, z] - coef * ((y_ahead(ez) - ez) - (ey_n - ey))
            hy = st[b + 4, z] - coef * ((ex_n - ex) - (x_ahead(ez) - ez))
            hz = st[b + 5, z] - coef * ((x_ahead(ey) - ey) - (y_ahead(ex) - ex))
            ex = ex + scale * ((hz - y_behind(hz)) - (hy - hy_p))
            ey = ey + scale * ((hx - hx_p) - (hz - x_behind(hz)))
            ez = ez + scale * ((hy - x_behind(hy)) - (hx - y_behind(hx)))
            st[b, z], st[b + 1, z], st[b + 2, z] = ex, ey, ez
            st[b + 3, z], st[b + 4, z], st[b + 5, z] = hx, hy, hz
            if weights is not None:
                own = z - 2 * depth
                for c, e in enumerate((ex, ey, ez)):
                    acc[0, 3 * r + c, own] = acc[0, 3 * r + c, own] + e * weights[0]
                    acc[1, 3 * r + c, own] = acc[1, 3 * r + c, own] - e * weights[1]
            carried.append((hx, hy))
        return tuple(carried)

    layers_all = n_blocks * depth
    for n in range(1, STEPS + 1):
        angle = omega_step * n
        weights = (math.cos(angle), math.sin(angle))
        zero = jnp.zeros((rows, nx), jnp.float32)
        carry = ((zero, zero), (zero, zero))
        carry = lax.fori_loop(n - 1, 2 * depth, lambda z, c: layer(z, c, None), carry)
        carry = lax.fori_loop(2 * depth, 3 * depth, lambda z, c: layer(z, c, weights), carry)
        lax.fori_loop(3 * depth, layers_all - n, lambda z, c: layer(z, c, None), carry)

    result = pltpu.make_async_copy(
        st.at[pl.ds(0, 12), pl.ds(2 * depth, depth), pl.ds(row_own, rows_own), :], out, sem_out
    )
    result.start()
    column_sum = jnp.zeros((rows, nx), jnp.float32)
    for own in range(depth):
        g = jnp.zeros((rows, nx), jnp.float32)
        for c in range(3):
            g = g + acc[0, c, own] * acc[0, 3 + c, own] - acc[1, c, own] * acc[1, 3 + c, own]
        in_layer = (info[8] + own >= 0) & (info[8] + own < info[9])
        column_sum = column_sum + jnp.where(in_layer, g, 0.0)
    sens = mm(row_table[...], mm(column_sum, col_table[...])) * (eps_span / (STEPS * 3 * depth))
    weighted = sens * slope[...]
    spectrum = mm(own_y[...], mm(weighted, basis_xt[...])) * response[...]
    share[...] = mm(basis_y[...], mm(spectrum, basis_x[...]))
    result.wait()


def body(fields, eps_inv, row_counts, col_counts, density):
    runs, comps, depth, rows_own, nx = fields.shape
    n_gz, n_gy = lax.axis_size("gz"), lax.axis_size("gy")
    gz, gy, core = lax.axis_index("gz"), lax.axis_index("gy"), lax.axis_index("col")
    index = gz * 2 + core
    n_z = n_gz * 2
    assert STEPS == 2 * depth and rows_own >= STEPS

    own = jnp.concatenate([fields.reshape(runs * comps, depth, rows_own, nx), (courant * eps_inv)[None]])

    def swap_core(x):
        return lax.ppermute(x, "col", [(0, 1), (1, 0)])

    def cross(x):
        pairs = []
        for c in range(n_gz - 1):
            a, b = 2 * c + 1, 2 * c + 2
            pairs += [(a, b), (b, a)]
        return lax.ppermute(x, Z, pairs)

    if n_gy == 2:
        rows = rows_own + STEPS
        row_own = gy * STEPS
        halo_at = [(1 - gy) * rows_own]
        ways = [{0: 1, 1: 0}]
        starts = [(1 - gy) * (rows_own - STEPS)]
    else:
        rows = rows_own + 2 * STEPS
        row_own = jnp.int32(STEPS)
        halo_at = [jnp.int32(0), jnp.int32(STEPS + rows_own)]
        ways = [{y: y + 1 for y in range(n_gy - 1)}, {y: y - 1 for y in range(1, n_gy)}]
        starts = [rows_own - STEPS, 0]
    sides = len(ways)

    def edge(x, s):
        return lax.dynamic_slice_in_dim(x, starts[s], STEPS, axis=2)

    def along_y(x, s):
        return lax.ppermute(x, "gy", list(ways[s].items()))

    def across(x, s):
        pairs = []
        for c in range(n_gz - 1):
            for y, to in ways[s].items():
                a, b = ((c, y, 1), (c + 1, to, 0)), ((c + 1, y, 0), (c, to, 1))
                for src, dst in (a, b):
                    pairs.append(tuple((p[0] * n_gy + p[1]) * 2 + p[2] for p in (src, dst)))
        return lax.ppermute(x, ("gz", "gy", "col"), pairs)

    sibling = swap_core(own)
    near = cross(own)
    far = cross(sibling)
    near_sib = swap_core(near)
    full = [far, near, own, sibling, near_sib]
    halos = []
    for s in range(sides):
        mine, theirs = edge(own, s), edge(sibling, s)
        y_own = along_y(mine, s)
        y_near = across(mine, s)
        y_far = across(theirs, s)
        halos.append([y_far, y_near, y_own, swap_core(y_own), swap_core(y_near)])

    layer_start = depth * n_z // 2 - depth - depth // 2
    info = [core, row_own]
    info += halo_at + [jnp.int32(0)] * (2 - sides)
    info += [2 * depth - index * depth, depth * n_z - index * depth + 2 * depth]
    info += [
        jnp.where(gy == 0, STEPS, 0) if sides == 2 else jnp.int32(0),
        jnp.where(gy == n_gy - 1, STEPS + rows_own, rows) if sides == 2 else jnp.int32(rows),
    ]
    info += [index * depth - layer_start, jnp.int32(3 * depth)]
    info = jnp.stack([jnp.asarray(v, jnp.int32) for v in info])

    band, design_cols = density.shape
    tall = band * n_gy
    place_y = jnp.arange(rows, dtype=jnp.int32)[:, None] - row_own
    row_table = band_table(row_counts[0], place_y).T
    col_table = band_table(col_counts, jnp.arange(nx, dtype=jnp.int32)[:, None])
    basis_x, wave_x = real_basis(design_cols)
    basis_y, wave_y = real_basis(tall)
    response = 1.0 / (
        1.0
        + FILTER_LEN**2
        * (
            4.0 * np.sin(math.pi * wave_y / tall)[:, None] ** 2
            + 4.0 * np.sin(math.pi * wave_x / design_cols)[None, :] ** 2
        )
    )
    const = lambda a: jnp.asarray(a, jnp.float32)
    own_y = lax.dynamic_slice_in_dim(const(basis_y), gy * band, band, 1)

    operands = [info] + full + [h for side in halos for h in side]
    operands += [row_table, col_table, slope_of(density), const(basis_x), const(basis_x.T), const(basis_y.T), own_y, const(response)]
    n_any = 5 * (1 + sides)
    anywhere = pl.BlockSpec(memory_space=pl.ANY)
    vmem = pl.BlockSpec(memory_space=pltpu.VMEM)
    fields_out, share = pl.pallas_call(
        functools.partial(window_kernel, (depth, rows_own, rows, sides, sides == 2)),
        out_shape=(
            jax.ShapeDtypeStruct((runs * comps, depth, rows_own, nx), jnp.float32),
            jax.ShapeDtypeStruct((tall, design_cols), jnp.float32),
        ),
        in_specs=[pl.BlockSpec(memory_space=pltpu.SMEM)] + [anywhere] * n_any + [vmem] * 8,
        out_specs=(anywhere, vmem),
        scratch_shapes=[
            pltpu.VMEM((PLANES, 5 * depth, rows, nx), jnp.float32),
            pltpu.VMEM((2, 6, depth, rows, nx), jnp.float32),
            pltpu.SemaphoreType.DMA((5,)),
            pltpu.SemaphoreType.DMA((sides, 5)),
            pltpu.SemaphoreType.DMA,
        ],
        compiler_params=pltpu.CompilerParams(vmem_limit_bytes=24 * 1024 * 1024),
        cost_estimate=pl.CostEstimate(flops=60_000_000, bytes_accessed=8_000_000, transcendentals=0),
    )(*operands)

    width = design_cols // n_z
    blocks = share.reshape(n_gy, band, n_gz, 2, width).transpose(2, 0, 3, 1, 4)
    blocks = blocks.reshape(n_gz * n_gy * 2, band, width)
    got = lax.all_to_all(blocks, ("gz", "gy", "col"), 0, 0)
    gradient = jnp.sum(got, axis=0)
    return fields_out.reshape(fields.shape), gradient


def solution(mesh):
    in_specs = (
        P("groups", None, ("gz", "col"), "gy", None),
        P(("groups", "gz", "col"), "gy", None),
        P(("groups", "gy"), None),
        P("groups"),
        P(("groups", "gy"), None),
    )
    out_specs = (P("groups", None, ("gz", "col"), "gy", None), P(("groups", "gy"), ("gz", "col")))
    return jax.shard_map(body, mesh=mesh, in_specs=in_specs, out_specs=out_specs, check_vma=False)
```

```python
import functools
import math

import jax
import jax.numpy as jnp
import numpy as np
from jax import lax
from jax.experimental import pallas as pl
from jax.experimental.pallas import tpu as pltpu
from jax.sharding import PartitionSpec as P

STEPS = 8
FILTER_LEN = 12

courant = 0.5
omega_step = 0.7
beta_proj = 4.0
eta_proj = 0.5
eps_span = 11.1
highest = lax.Precision.HIGHEST

Z = ("gz", "col")
HALF = STEPS // 2


def slope_of(density):
    norm = math.tanh(beta_proj * eta_proj) + math.tanh(beta_proj * (1.0 - eta_proj))
    bent = jnp.tanh(beta_proj * (density - eta_proj))
    return beta_proj * (1.0 - bent * bent) / norm


def real_basis(size):
    place = np.arange(size)
    rows, waves = [], []
    for k in range(size // 2 + 1):
        angle = 2.0 * np.pi * ((k * place) % size) / size
        edge = k == 0 or 2 * k == size
        rows.append(np.cos(angle) * math.sqrt((1.0 if edge else 2.0) / size))
        waves.append(k)
        if not edge:
            rows.append(np.sin(angle) * math.sqrt(2.0 / size))
            waves.append(k)
    return np.array(rows), np.array(waves)


def band_table(counts, place):
    ends = jnp.cumsum(counts)
    starts = ends - counts
    return ((place >= starts[None, :]) & (place < ends[None, :])).astype(jnp.float32)


def mm(left, right):
    return jnp.dot(left, right, precision=highest, preferred_element_type=jnp.float32)


def strip_of(block, up):
    low_half = lax.broadcasted_iota(jnp.int32, (8, 128), 0) < HALF
    rows = block.shape[0]
    if up:
        a, b = block[rows - 8 :, :128], block[rows - 8 :, 128:]
        return jnp.where(low_half, pltpu.roll(a, HALF, 0), b)
    a, b = block[:8, :128], block[:8, 128:]
    return jnp.where(low_half, a, pltpu.roll(b, HALF, 0))


def strips_of(block, info, sides):
    if sides == 2:
        return [strip_of(block, True), strip_of(block, False)]
    return [jnp.where(info[1] == 0, strip_of(block, True), strip_of(block, False))]


def edge_kernel(sides, info, fields, eps, scaled, *strips):
    for l in range(eps.shape[0]):
        scale = courant * eps[l]
        scaled[l] = scale
        for c in range(13):
            block = fields[c, l] if c < 12 else scale
            for s, strip in enumerate(strips_of(block, info, sides)):
                strips[s][c, l] = strip


def window_kernel(cfg, *refs):
    depth, rows_own, sides, second = cfg
    it = iter(refs)
    take = lambda n: [next(it) for _ in range(n)]
    info = next(it)
    full = take(3)
    strip_in = [take(3) for _ in range(sides)]
    if second:
        (scale_in, acc_in) = take(2)
        row_table, col_table, slope, basis_x, basis_xt, basis_y, own_y, response = take(8)
        out, share = take(2)
    else:
        eps_full = take(3)
        out, scale_out, acc_out = take(3)
        strip_out = take(sides)
    if second:
        st, strips, acc, sem_full, sem_strip, sem_out = take(6)
        scale_ref = scale_in
    else:
        st, strips, sem_full, sem_strip, sem_eps, sem_out = take(6)
        scale_ref = scale_out
        acc = acc_out

    core, gy = info[0], info[1]
    copies = []
    for b in range(3):
        place = jnp.where(core == 0, b * depth, (2 - b) * depth)
        layers = pl.ds(place, depth)
        copies.append(pltpu.make_async_copy(full[b], st.at[:, layers, pl.ds(0, rows_own), :], sem_full.at[b]))
        for s in range(sides):
            copies.append(pltpu.make_async_copy(strip_in[s][b], strips.at[s, :, layers], sem_strip.at[s, b]))
        if not second:
            copies.append(
                pltpu.make_async_copy(eps_full[b], scale_ref.at[layers, pl.ds(0, rows_own), :], sem_eps.at[b])
            )
    for copy in copies:
        copy.start()
    for copy in copies:
        copy.wait()

    nx = st.shape[-1]
    rows = st.shape[-2]
    low_half = lax.broadcasted_iota(jnp.int32, (8, 128), 0) < HALF
    low_half_at = jnp.where(low_half, 0, 1)
    n_layers = 3 * depth
    planes = 12 if second else 13
    for c in range(planes):
        for l in range(n_layers):
            if sides == 2:
                lo, hi = strips[0, c, l], strips[1, c, l]
                left = jnp.where(low_half, hi, pltpu.roll(lo, HALF, 0))
                right = jnp.where(low_half, pltpu.roll(hi, HALF, 0), lo)
            else:
                v = strips[0, c, l]
                w = pltpu.roll(v, HALF, 0)
                keep = low_half_at == gy
                left = jnp.where(keep, jnp.where(low_half, v, w), 0.0)
                right = jnp.where(keep, jnp.where(low_half, w, v), 0.0)
            tile = jnp.concatenate([left, right], axis=1)
            if c == 12:
                scale_ref[l, rows_own:rows, :] = tile
            else:
                st[c, l, rows_own:rows, :] = tile

    row_at = lax.broadcasted_iota(jnp.int32, (rows, nx), 0)
    lane_at = lax.broadcasted_iota(jnp.int32, (rows, 128), 1)
    last_lane, first_lane = lane_at == 127, lane_at == 0
    ahead = jnp.where(info[4] > 0, courant, 0.0)
    behind = jnp.where(info[5] > 0, courant, 0.0)
    coef_in = jnp.where(row_at < rows_own, courant, jnp.where(row_at < rows_own + HALF, ahead, behind))
    low_layer, high_layer = info[2], info[3]

    def y_ahead(f):
        return pltpu.roll(f, rows - 1, 0)

    def y_behind(f):
        return pltpu.roll(f, 1, 0)

    def x_ahead(f):
        a, b = pltpu.roll(f[:, :128], 127, 1), pltpu.roll(f[:, 128:], 127, 1)
        return jnp.concatenate([jnp.where(last_lane, b, a), jnp.where(last_lane, 0.0, b)], axis=1)

    def x_behind(f):
        a, b = pltpu.roll(f[:, :128], 1, 1), pltpu.roll(f[:, 128:], 1, 1)
        return jnp.concatenate([jnp.where(first_lane, 0.0, a), jnp.where(first_lane, a, b)], axis=1)

    for m in range(1, HALF + 1):
        angle = omega_step * (m + (HALF if second else 0))
        w_re, w_im = math.cos(angle), math.sin(angle)
        prev = [None, None]
        for z in range(m - 1, n_layers - m):
            coef = coef_in * jnp.where((z >= low_layer) & (z < high_layer), 1.0, 0.0)
            scale = scale_ref[z]
            for r in range(2):
                b = 6 * r
                ex, ey, ez = st[b, z], st[b + 1, z], st[b + 2, z]
                ex_n, ey_n = st[b, z + 1], st[b + 1, z + 1]
                hx = st[b + 3, z] - coef * ((y_ahead(ez) - ez) - (ey_n - ey))
                hy = st[b + 4, z] - coef * ((ex_n - ex) - (x_ahead(ez) - ez))
                if z >= m:
                    hx_p, hy_p = prev[r]
                    hz = st[b + 5, z] - coef * ((x_ahead(ey) - ey) - (y_ahead(ex) - ex))
                    ex = ex + scale * ((hz - y_behind(hz)) - (hy - hy_p))
                    ey = ey + scale * ((hx - hx_p) - (hz - x_behind(hz)))
                    ez = ez + scale * ((hy - x_behind(hy)) - (hx - y_behind(hx)))
                    st[b, z], st[b + 1, z], st[b + 2, z] = ex, ey, ez
                    st[b + 3, z], st[b + 4, z], st[b + 5, z] = hx, hy, hz
                    own = z - depth
                    if 0 <= own < depth:
                        for c, e in enumerate((ex, ey, ez)):
                            e = e[:rows_own]
                            re, im = e * w_re, e * w_im
                            if m > 1:
                                acc[0, 3 * r + c, own] = acc[0, 3 * r + c, own] + re
                                acc[1, 3 * r + c, own] = acc[1, 3 * r + c, own] - im
                            elif second:
                                acc[0, 3 * r + c, own] = acc_in[0, 3 * r + c, own] + re
                                acc[1, 3 * r + c, own] = acc_in[1, 3 * r + c, own] - im
                            else:
                                acc[0, 3 * r + c, own] = re
                                acc[1, 3 * r + c, own] = -im
                else:
                    st[b + 3, z], st[b + 4, z] = hx, hy
                prev[r] = (hx, hy)

    result = pltpu.make_async_copy(st.at[:, pl.ds(depth, depth), pl.ds(0, rows_own), :], out, sem_out)
    result.start()
    if not second:
        for c in range(12):
            for l in range(depth):
                for s, strip in enumerate(strips_of(st[c, depth + l, :rows_own, :], info, sides)):
                    strip_out[s][c, l] = strip
    else:
        column_sum = jnp.zeros((rows_own, nx), jnp.float32)
        for own in range(depth):
            g = jnp.zeros((rows_own, nx), jnp.float32)
            for c in range(3):
                g = g + acc[0, c, own] * acc[0, 3 + c, own] - acc[1, c, own] * acc[1, 3 + c, own]
            in_layer = (info[6] + own >= 0) & (info[6] + own < 3 * depth)
            column_sum = column_sum + jnp.where(in_layer, g, 0.0)
        sens = mm(row_table[...], mm(column_sum, col_table[...])) * (eps_span / (STEPS * 3 * depth))
        weighted = sens * slope[...]
        spectrum = mm(own_y[...], mm(weighted, basis_xt[...])) * response[...]
        share[...] = mm(basis_y[...], mm(spectrum, basis_x[...]))
    result.wait()


def body(fields, eps_inv, row_counts, col_counts, density):
    runs, comps, depth, rows_own, nx = fields.shape
    n_gz, n_gy = lax.axis_size("gz"), lax.axis_size("gy")
    gz, gy, core = lax.axis_index("gz"), lax.axis_index("gy"), lax.axis_index("col")
    index = gz * 2 + core
    n_z = n_gz * 2
    assert HALF == depth and rows_own == 16 and nx == 256
    rows = rows_own + 2 * HALF
    own = fields.reshape(runs * comps, depth, rows_own, nx)

    def swap_core(x):
        return lax.ppermute(x, "col", [(0, 1), (1, 0)])

    def cross(x):
        pairs = []
        for c in range(n_gz - 1):
            a, b = 2 * c + 1, 2 * c + 2
            pairs += [(a, b), (b, a)]
        return lax.ppermute(x, Z, pairs)

    if n_gy == 2:
        ways = [{0: 1, 1: 0}]
    else:
        ways = [{y: y + 1 for y in range(n_gy - 1)}, {y: y - 1 for y in range(1, n_gy)}]
    sides = len(ways)

    def along_y(x, s):
        return lax.ppermute(x, "gy", list(ways[s].items()))

    def across(x, s):
        pairs = []
        for c in range(n_gz - 1):
            for y, to in ways[s].items():
                for src, dst in (((c, y, 1), (c + 1, to, 0)), ((c + 1, y, 0), (c, to, 1))):
                    pairs.append(tuple((p[0] * n_gy + p[1]) * 2 + p[2] for p in (src, dst)))
        return lax.ppermute(x, ("gz", "gy", "col"), pairs)

    layer_start = depth * n_z // 2 - depth - depth // 2
    info = [
        core,
        gy,
        depth - index * depth,
        depth * n_z - index * depth + depth,
        jnp.where(gy < n_gy - 1, 1, 0),
        jnp.where(gy > 0, 1, 0),
        index * depth - layer_start,
    ]
    info = jnp.stack([jnp.asarray(v, jnp.int32) for v in info])

    anywhere = pl.BlockSpec(memory_space=pl.ANY)
    vmem = pl.BlockSpec(memory_space=pltpu.VMEM)
    smem = pl.BlockSpec(memory_space=pltpu.SMEM)
    shape = lambda *s: jax.ShapeDtypeStruct(s, jnp.float32)
    limit = pltpu.CompilerParams(vmem_limit_bytes=24 * 1024 * 1024)

    def strips_sent(strips):
        sent = []
        for s, strip in enumerate(strips):
            mine = along_y(strip, s)
            sent += [across(strip, s), mine, swap_core(mine)]
        return sent

    full = [cross(own), own, swap_core(own)]
    scaled, *strips = pl.pallas_call(
        functools.partial(edge_kernel, sides),
        out_shape=(shape(depth, rows_own, nx),) + (shape(13, depth, 8, 128),) * sides,
        in_specs=[smem, vmem, vmem],
        out_specs=(vmem,) * (1 + sides),
        compiler_params=limit,
    )(info, own, eps_inv)
    operands = [info] + full + strips_sent(strips) + [cross(scaled), scaled, swap_core(scaled)]
    cost = pl.CostEstimate(flops=20_000_000, bytes_accessed=4_000_000, transcendentals=0)
    state, scale, acc, *strips = pl.pallas_call(
        functools.partial(window_kernel, (depth, rows_own, sides, False)),
        out_shape=(
            shape(runs * comps, depth, rows_own, nx),
            shape(3 * depth, rows, nx),
            shape(2, 6, depth, rows_own, nx),
        )
        + (shape(12, depth, 8, 128),) * sides,
        in_specs=[smem] + [anywhere] * (6 + 3 * sides),
        out_specs=(anywhere, vmem, vmem) + (vmem,) * sides,
        scratch_shapes=[
            pltpu.VMEM((12, 3 * depth, rows, nx), jnp.float32),
            pltpu.VMEM((sides, 13, 3 * depth, 8, 128), jnp.float32),
            pltpu.SemaphoreType.DMA((3,)),
            pltpu.SemaphoreType.DMA((sides, 3)),
            pltpu.SemaphoreType.DMA((3,)),
            pltpu.SemaphoreType.DMA,
        ],
        compiler_params=limit,
        cost_estimate=cost,
    )(*operands)

    band, design_cols = density.shape
    tall = band * n_gy
    row_table = band_table(row_counts[0], jnp.arange(rows_own, dtype=jnp.int32)[:, None]).T
    col_table = band_table(col_counts, jnp.arange(nx, dtype=jnp.int32)[:, None])
    basis_x, wave_x = real_basis(design_cols)
    basis_y, wave_y = real_basis(tall)
    response = 1.0 / (
        1.0
        + FILTER_LEN**2
        * (
            4.0 * np.sin(math.pi * wave_y / tall)[:, None] ** 2
            + 4.0 * np.sin(math.pi * wave_x / design_cols)[None, :] ** 2
        )
    )
    const = lambda a: jnp.asarray(a, jnp.float32)
    own_y = lax.dynamic_slice_in_dim(const(basis_y), gy * band, band, 1)
    operands = [info, cross(state), state, swap_core(state)] + strips_sent(strips) + [scale, acc]
    operands += [row_table, col_table, slope_of(density), const(basis_x), const(basis_x.T), const(basis_y.T), own_y, const(response)]
    fields_out, share = pl.pallas_call(
        functools.partial(window_kernel, (depth, rows_own, sides, True)),
        out_shape=(shape(runs * comps, depth, rows_own, nx), shape(tall, design_cols)),
        in_specs=[smem] + [anywhere] * (3 + 3 * sides) + [vmem] * 10,
        out_specs=(anywhere, vmem),
        scratch_shapes=[
            pltpu.VMEM((12, 3 * depth, rows, nx), jnp.float32),
            pltpu.VMEM((sides, 12, 3 * depth, 8, 128), jnp.float32),
            pltpu.VMEM((2, 6, depth, rows_own, nx), jnp.float32),
            pltpu.SemaphoreType.DMA((3,)),
            pltpu.SemaphoreType.DMA((sides, 3)),
            pltpu.SemaphoreType.DMA,
        ],
        compiler_params=limit,
        cost_estimate=cost,
    )(*operands)

    width = design_cols // n_z
    blocks = share.reshape(n_gy, band, n_gz, 2, width).transpose(2, 0, 3, 1, 4)
    blocks = blocks.reshape(n_gz * n_gy * 2, band, width)
    got = lax.all_to_all(blocks, ("gz", "gy", "col"), 0, 0)
    gradient = jnp.sum(got, axis=0)
    return fields_out.reshape(fields.shape), gradient


def solution(mesh):
    in_specs = (
        P("groups", None, ("gz", "col"), "gy", None),
        P(("groups", "gz", "col"), "gy", None),
        P(("groups", "gy"), None),
        P("groups"),
        P(("groups", "gy"), None),
    )
    out_specs = (P("groups", None, ("gz", "col"), "gy", None), P(("groups", "gy"), ("gz", "col")))
    return jax.shard_map(body, mesh=mesh, in_specs=in_specs, out_specs=out_specs, check_vma=False)
```

```python
import functools
import math

import jax
import jax.numpy as jnp
import numpy as np
from jax import lax
from jax.experimental import pallas as pl
from jax.experimental.pallas import tpu as pltpu
from jax.sharding import PartitionSpec as P

STEPS = 8
FILTER_LEN = 12

courant = 0.5
omega_step = 0.7
beta_proj = 4.0
eta_proj = 0.5
eps_span = 11.1
highest = lax.Precision.HIGHEST

Z = ("gz", "col")
HALF = STEPS // 2


def slope_of(density):
    norm = math.tanh(beta_proj * eta_proj) + math.tanh(beta_proj * (1.0 - eta_proj))
    bent = jnp.tanh(beta_proj * (density - eta_proj))
    return beta_proj * (1.0 - bent * bent) / norm


def real_basis(size):
    place = np.arange(size)
    rows, waves = [], []
    for k in range(size // 2 + 1):
        angle = 2.0 * np.pi * ((k * place) % size) / size
        edge = k == 0 or 2 * k == size
        rows.append(np.cos(angle) * math.sqrt((1.0 if edge else 2.0) / size))
        waves.append(k)
        if not edge:
            rows.append(np.sin(angle) * math.sqrt(2.0 / size))
            waves.append(k)
    return np.array(rows), np.array(waves)


def band_table(counts, place):
    ends = jnp.cumsum(counts)
    starts = ends - counts
    return ((place >= starts[None, :]) & (place < ends[None, :])).astype(jnp.float32)


def mm(left, right):
    return jnp.dot(left, right, precision=highest, preferred_element_type=jnp.float32)


def strip_of(tile, up):
    low_half = lax.broadcasted_iota(jnp.int32, (8, 128), 0) < HALF
    a, b = tile[:, :128], tile[:, 128:]
    if up:
        return jnp.where(low_half, pltpu.roll(a, HALF, 0), b)
    return jnp.where(low_half, a, pltpu.roll(b, HALF, 0))


def edge_kernel(depth, rows_own, sides, info, fields, eps, *refs):
    strips, tiles, sems = refs[:sides], refs[sides], refs[sides + 1]
    gy = info[1]
    copies = []
    for s in range(sides):
        at = rows_own - 8 if s == 0 else 0
        if sides == 1:
            at = pl.multiple_of((1 - gy) * (rows_own - 8), 8)
        rows = pl.ds(at, 8)
        copies.append(pltpu.make_async_copy(fields.at[:, :, rows, :], tiles.at[s, pl.ds(0, 12)], sems.at[s, 0]))
        copies.append(pltpu.make_async_copy(eps.at[:, rows, :], tiles.at[s, 12], sems.at[s, 1]))
    for copy in copies:
        copy.start()
    for copy in copies:
        copy.wait()
    for s in range(sides):
        for c in range(13):
            for l in range(depth):
                tile = tiles[s, c, l]
                if sides == 2:
                    strips[s][c, l] = strip_of(tile, s == 0)
                else:
                    strips[s][c, l] = jnp.where(gy == 0, strip_of(tile, True), strip_of(tile, False))


def window_kernel(cfg, *refs):
    depth, rows_own, sides, second = cfg
    it = iter(refs)
    take = lambda n: [next(it) for _ in range(n)]
    info = next(it)
    full = take(3)
    strip_in = [take(3) for _ in range(sides)]
    if second:
        (scale_ref, acc_in) = take(2)
        row_table, col_table, slope, basis_x, basis_xt, basis_y, own_y, response = take(8)
        out, share = take(2)
        st, strips, acc, done, sem_full, sem_strip, sem_out = take(7)
    else:
        eps_full = take(3)
        done, scale_ref, acc = take(3)
        strip_out = take(sides)
        st, strips, eps, sem_full, sem_strip, sem_eps = take(6)

    core, gy = info[0], info[1]

    def copies_of(b, place):
        layers = pl.ds(place * depth, depth)
        found = [pltpu.make_async_copy(full[b], st.at[:, layers, pl.ds(0, rows_own), :], sem_full.at[place])]
        for s in range(sides):
            found.append(pltpu.make_async_copy(strip_in[s][b], strips.at[s, :, layers], sem_strip.at[s, place]))
        if not second:
            found.append(pltpu.make_async_copy(eps_full[b], eps.at[layers], sem_eps.at[place]))
        return found

    @pl.when(core == 0)
    def _():
        for b in range(3):
            for copy in copies_of(b, b):
                copy.start()

    @pl.when(core != 0)
    def _():
        for b in (2, 1, 0):
            for copy in copies_of(b, 2 - b):
                copy.start()

    nx = st.shape[-1]
    rows = st.shape[-2]
    low_half = lax.broadcasted_iota(jnp.int32, (8, 128), 0) < HALF
    low_half_at = jnp.where(low_half, 0, 1)
    n_layers = 3 * depth

    def arrive(place):
        for copy in copies_of(place, place):
            copy.wait()
        for l in range(place * depth, (place + 1) * depth):
            for c in range(12 if second else 13):
                if sides == 2:
                    lo, hi = strips[0, c, l], strips[1, c, l]
                    left = jnp.where(low_half, hi, pltpu.roll(lo, HALF, 0))
                    right = jnp.where(low_half, pltpu.roll(hi, HALF, 0), lo)
                else:
                    v = strips[0, c, l]
                    w = pltpu.roll(v, HALF, 0)
                    keep = low_half_at == gy
                    left = jnp.where(keep, jnp.where(low_half, v, w), 0.0)
                    right = jnp.where(keep, jnp.where(low_half, w, v), 0.0)
                tile = jnp.concatenate([left, right], axis=1)
                if c == 12:
                    scale_ref[l, rows_own:rows, :] = courant * tile
                    scale_ref[l, :rows_own, :] = courant * eps[l]
                else:
                    st[c, l, rows_own:rows, :] = tile

    row_at = lax.broadcasted_iota(jnp.int32, (rows, nx), 0)
    lane_at = lax.broadcasted_iota(jnp.int32, (rows, 128), 1)
    last_lane, first_lane = lane_at == 127, lane_at == 0
    ahead = jnp.where(info[4] > 0, courant, 0.0)
    behind = jnp.where(info[5] > 0, courant, 0.0)
    coef_in = jnp.where(row_at < rows_own, courant, jnp.where(row_at < rows_own + HALF, ahead, behind))
    low_layer, high_layer = info[2], info[3]

    def y_ahead(f):
        return pltpu.roll(f, rows - 1, 0)

    def y_behind(f):
        return pltpu.roll(f, 1, 0)

    def x_ahead(f):
        a, b = pltpu.roll(f[:, :128], 127, 1), pltpu.roll(f[:, 128:], 127, 1)
        return jnp.concatenate([jnp.where(last_lane, b, a), jnp.where(last_lane, 0.0, b)], axis=1)

    def x_behind(f):
        a, b = pltpu.roll(f[:, :128], 1, 1), pltpu.roll(f[:, 128:], 1, 1)
        return jnp.concatenate([jnp.where(first_lane, 0.0, a), jnp.where(first_lane, a, b)], axis=1)

    for m in range(1, HALF + 1):
        angle = omega_step * (m + (HALF if second else 0))
        w_re, w_im = math.cos(angle), math.sin(angle)
        prev = [None, None]
        for z in range(m - 1, n_layers - m):
            if m == 1 and z == 0:
                arrive(0)
            if m == 1 and (z + 1) % depth == 0:
                arrive((z + 1) // depth)
            coef = coef_in * jnp.where((z >= low_layer) & (z < high_layer), 1.0, 0.0)
            scale = scale_ref[z]
            own = z - depth
            for r in range(2):
                b = 6 * r
                ex, ey, ez = st[b, z], st[b + 1, z], st[b + 2, z]
                ex_n, ey_n = st[b, z + 1], st[b + 1, z + 1]
                hx = st[b + 3, z] - coef * ((y_ahead(ez) - ez) - (ey_n - ey))
                hy = st[b + 4, z] - coef * ((ex_n - ex) - (x_ahead(ez) - ez))
                if z >= m:
                    hx_p, hy_p = prev[r]
                    hz = st[b + 5, z] - coef * ((x_ahead(ey) - ey) - (y_ahead(ex) - ex))
                    ex = ex + scale * ((hz - y_behind(hz)) - (hy - hy_p))
                    ey = ey + scale * ((hx - hx_p) - (hz - x_behind(hz)))
                    ez = ez + scale * ((hy - x_behind(hy)) - (hx - y_behind(hx)))
                    for c, f in enumerate((ex, ey, ez, hx, hy, hz)):
                        if m < HALF:
                            st[b + c, z] = f
                            continue
                        done[b + c, own] = f[:rows_own]
                        if not second:
                            up, down = f[rows_own - 8 : rows_own], f[:8]
                            if sides == 2:
                                strip_out[0][b + c, own] = strip_of(up, True)
                                strip_out[1][b + c, own] = strip_of(down, False)
                            else:
                                strip_out[0][b + c, own] = jnp.where(
                                    gy == 0, strip_of(up, True), strip_of(down, False)
                                )
                    if 0 <= own < depth:
                        for c, e in enumerate((ex, ey, ez)):
                            e = e[:rows_own]
                            re, im = e * w_re, e * w_im
                            if m > 1:
                                acc[0, 3 * r + c, own] = acc[0, 3 * r + c, own] + re
                                acc[1, 3 * r + c, own] = acc[1, 3 * r + c, own] - im
                            elif second:
                                acc[0, 3 * r + c, own] = acc_in[0, 3 * r + c, own] + re
                                acc[1, 3 * r + c, own] = acc_in[1, 3 * r + c, own] - im
                            else:
                                acc[0, 3 * r + c, own] = re
                                acc[1, 3 * r + c, own] = -im
                else:
                    st[b + 3, z], st[b + 4, z] = hx, hy
                prev[r] = (hx, hy)

    if second:
        result = pltpu.make_async_copy(done, out, sem_out)
        result.start()
        column_sum = jnp.zeros((rows_own, nx), jnp.float32)
        for own in range(depth):
            g = jnp.zeros((rows_own, nx), jnp.float32)
            for c in range(3):
                g = g + acc[0, c, own] * acc[0, 3 + c, own] - acc[1, c, own] * acc[1, 3 + c, own]
            in_layer = (info[6] + own >= 0) & (info[6] + own < 3 * depth)
            column_sum = column_sum + jnp.where(in_layer, g, 0.0)
        sens = mm(row_table[...], mm(column_sum, col_table[...])) * (eps_span / (STEPS * 3 * depth))
        weighted = sens * slope[...]
        spectrum = mm(own_y[...], mm(weighted, basis_xt[...])) * response[...]
        shares = mm(basis_y[...], mm(spectrum, basis_x[...]))
        count, band, _ = share.shape
        n_gy = shares.shape[0] // band
        for d in range(count):
            y = d // 2 % n_gy
            share[d] = shares[y * band : (y + 1) * band]
        result.wait()


def sum_kernel(info, got, out):
    total = got[0]
    for d in range(1, got.shape[0]):
        total = total + got[d]
    width = out.shape[1]
    columns = total.shape[1]
    out[...] = pltpu.roll(total, lax.rem(columns - info[7], columns), 1)[:, :width]


def body(fields, eps_inv, row_counts, col_counts, density):
    runs, comps, depth, rows_own, nx = fields.shape
    n_gz, n_gy = lax.axis_size("gz"), lax.axis_size("gy")
    gz, gy, core = lax.axis_index("gz"), lax.axis_index("gy"), lax.axis_index("col")
    index = gz * 2 + core
    n_z = n_gz * 2
    assert HALF == depth and rows_own == 16 and nx == 256
    rows = rows_own + 2 * HALF
    own = fields.reshape(runs * comps, depth, rows_own, nx)

    def swap_core(x):
        return lax.ppermute(x, "col", [(0, 1), (1, 0)])

    def cross(x):
        pairs = []
        for c in range(n_gz - 1):
            a, b = 2 * c + 1, 2 * c + 2
            pairs += [(a, b), (b, a)]
        return lax.ppermute(x, Z, pairs)

    if n_gy == 2:
        ways = [{0: 1, 1: 0}]
    else:
        ways = [{y: y + 1 for y in range(n_gy - 1)}, {y: y - 1 for y in range(1, n_gy)}]
    sides = len(ways)

    def along_y(x, s):
        return lax.ppermute(x, "gy", list(ways[s].items()))

    layer_start = depth * n_z // 2 - depth - depth // 2
    info = [
        core,
        gy,
        depth - index * depth,
        depth * n_z - index * depth + depth,
        jnp.where(gy < n_gy - 1, 1, 0),
        jnp.where(gy > 0, 1, 0),
        index * depth - layer_start,
        index * (density.shape[1] // n_z),
    ]
    info = jnp.stack([jnp.asarray(v, jnp.int32) for v in info])

    anywhere = pl.BlockSpec(memory_space=pl.ANY)
    vmem = pl.BlockSpec(memory_space=pltpu.VMEM)
    smem = pl.BlockSpec(memory_space=pltpu.SMEM)
    shape = lambda *s: jax.ShapeDtypeStruct(s, jnp.float32)
    limit = pltpu.CompilerParams(vmem_limit_bytes=24 * 1024 * 1024)

    def strips_sent(strips):
        sent = []
        for s, strip in enumerate(strips):
            mine = along_y(strip, s)
            sent += [cross(mine), mine, swap_core(mine)]
        return sent

    strips = pl.pallas_call(
        functools.partial(edge_kernel, depth, rows_own, sides),
        out_shape=(shape(13, depth, 8, 128),) * sides,
        in_specs=[smem, anywhere, anywhere],
        out_specs=(vmem,) * sides,
        scratch_shapes=[
            pltpu.VMEM((sides, 13, depth, 8, nx), jnp.float32),
            pltpu.SemaphoreType.DMA((sides, 2)),
        ],
        compiler_params=limit,
    )(info, own, eps_inv)
    operands = [info, cross(own), own, swap_core(own)] + strips_sent(strips)
    operands += [cross(eps_inv), eps_inv, swap_core(eps_inv)]
    cost = pl.CostEstimate(flops=20_000_000, bytes_accessed=4_000_000, transcendentals=0)
    window = pltpu.VMEM((12, 3 * depth, rows, nx), jnp.float32)
    block = pltpu.VMEM((12, depth, rows_own, nx), jnp.float32)
    arrivals = [pltpu.SemaphoreType.DMA((3,)), pltpu.SemaphoreType.DMA((sides, 3))]
    state, scale, acc, *strips = pl.pallas_call(
        functools.partial(window_kernel, (depth, rows_own, sides, False)),
        out_shape=(
            shape(runs * comps, depth, rows_own, nx),
            shape(3 * depth, rows, nx),
            shape(2, 6, depth, rows_own, nx),
        )
        + (shape(12, depth, 8, 128),) * sides,
        in_specs=[smem] + [anywhere] * (6 + 3 * sides),
        out_specs=(vmem, vmem, vmem) + (vmem,) * sides,
        scratch_shapes=[
            window,
            pltpu.VMEM((sides, 13, 3 * depth, 8, 128), jnp.float32),
            pltpu.VMEM((3 * depth, rows_own, nx), jnp.float32),
        ]
        + arrivals
        + [pltpu.SemaphoreType.DMA((3,))],
        compiler_params=limit,
        cost_estimate=cost,
    )(*operands)

    band, design_cols = density.shape
    tall = band * n_gy
    row_table = band_table(row_counts[0], jnp.arange(rows_own, dtype=jnp.int32)[:, None]).T
    col_table = band_table(col_counts, jnp.arange(nx, dtype=jnp.int32)[:, None])
    basis_x, wave_x = real_basis(design_cols)
    basis_y, wave_y = real_basis(tall)
    response = 1.0 / (
        1.0
        + FILTER_LEN**2
        * (
            4.0 * np.sin(math.pi * wave_y / tall)[:, None] ** 2
            + 4.0 * np.sin(math.pi * wave_x / design_cols)[None, :] ** 2
        )
    )
    const = lambda a: jnp.asarray(a, jnp.float32)
    own_y = lax.dynamic_slice_in_dim(const(basis_y), gy * band, band, 1)
    operands = [info, cross(state), state, swap_core(state)] + strips_sent(strips) + [scale, acc]
    operands += [row_table, col_table, slope_of(density), const(basis_x), const(basis_x.T), const(basis_y.T), own_y, const(response)]
    n_all = n_z * n_gy
    fields_out, share = pl.pallas_call(
        functools.partial(window_kernel, (depth, rows_own, sides, True)),
        out_shape=(shape(runs * comps, depth, rows_own, nx), shape(n_all, band, design_cols)),
        in_specs=[smem] + [anywhere] * (3 + 3 * sides) + [vmem] * 10,
        out_specs=(anywhere, vmem),
        scratch_shapes=[
            window,
            pltpu.VMEM((sides, 12, 3 * depth, 8, 128), jnp.float32),
            pltpu.VMEM((2, 6, depth, rows_own, nx), jnp.float32),
            block,
        ]
        + arrivals
        + [pltpu.SemaphoreType.DMA],
        compiler_params=limit,
        cost_estimate=cost,
    )(*operands)

    got = lax.all_to_all(share, ("gz", "gy", "col"), 0, 0)
    gradient = pl.pallas_call(
        sum_kernel,
        out_shape=shape(band, design_cols // n_z),
        in_specs=[smem, vmem],
        out_specs=vmem,
    )(info, got)
    return fields_out.reshape(fields.shape), gradient


def solution(mesh):
    in_specs = (
        P("groups", None, ("gz", "col"), "gy", None),
        P(("groups", "gz", "col"), "gy", None),
        P(("groups", "gy"), None),
        P("groups"),
        P(("groups", "gy"), None),
    )
    out_specs = (P("groups", None, ("gz", "col"), "gy", None), P(("groups", "gy"), ("gz", "col")))
    return jax.shard_map(body, mesh=mesh, in_specs=in_specs, out_specs=out_specs, check_vma=False)
```

```python
import functools
import math

import jax
import jax.numpy as jnp
import numpy as np
from jax import lax
from jax.experimental import pallas as pl
from jax.experimental.pallas import tpu as pltpu
from jax.sharding import PartitionSpec as P

STEPS = 8
FILTER_LEN = 12

courant = 0.5
omega_step = 0.7
beta_proj = 4.0
eta_proj = 0.5
eps_span = 11.1
highest = lax.Precision.HIGHEST

Z = ("gz", "col")
HALF = STEPS // 2


def slope_of(density):
    norm = math.tanh(beta_proj * eta_proj) + math.tanh(beta_proj * (1.0 - eta_proj))
    bent = jnp.tanh(beta_proj * (density - eta_proj))
    return beta_proj * (1.0 - bent * bent) / norm


def real_basis(size):
    place = np.arange(size)
    rows, waves = [], []
    for k in range(size // 2 + 1):
        angle = 2.0 * np.pi * ((k * place) % size) / size
        edge = k == 0 or 2 * k == size
        rows.append(np.cos(angle) * math.sqrt((1.0 if edge else 2.0) / size))
        waves.append(k)
        if not edge:
            rows.append(np.sin(angle) * math.sqrt(2.0 / size))
            waves.append(k)
    return np.array(rows), np.array(waves)


def band_table(counts, place):
    ends = jnp.cumsum(counts)
    starts = ends - counts
    return ((place >= starts[None, :]) & (place < ends[None, :])).astype(jnp.float32)


def mm(left, right):
    return jnp.dot(left, right, precision=highest, preferred_element_type=jnp.float32)


def strip_of(tile, up):
    low_half = lax.broadcasted_iota(jnp.int32, (8, 128), 0) < HALF
    a, b = tile[:, :128], tile[:, 128:]
    if up:
        return jnp.where(low_half, pltpu.roll(a, HALF, 0), b)
    return jnp.where(low_half, a, pltpu.roll(b, HALF, 0))


def window_kernel(cfg, *refs):
    depth, rows_own, sides, second = cfg
    it = iter(refs)
    take = lambda n: [next(it) for _ in range(n)]
    info = next(it)
    full = take(3)
    strip_in = [take(3) for _ in range(sides)]
    if second:
        (scale_ref, acc_in) = take(2)
        row_table, col_table, slope, basis_x, basis_xt, basis_y, own_y, response = take(8)
        out, share = take(2)
        st, strips, acc, done, sem_full, sem_strip, sem_out = take(7)
    else:
        done, scale_ref, acc = take(3)
        strip_out = take(sides)
        st, strips, sem_full, sem_strip = take(4)

    core, gy = info[0], info[1]

    def copies_of(b, place):
        layers = pl.ds(place * depth, depth)
        found = [pltpu.make_async_copy(full[b], st.at[:, layers, pl.ds(0, rows_own), :], sem_full.at[place])]
        for s in range(sides):
            planes = pl.ds(0, strip_in[s][b].shape[0])
            found.append(pltpu.make_async_copy(strip_in[s][b], strips.at[s, planes, layers], sem_strip.at[s, place]))
        return found

    @pl.when(core == 0)
    def _():
        for b in range(3):
            for copy in copies_of(b, b):
                copy.start()

    @pl.when(core != 0)
    def _():
        for b in (2, 1, 0):
            for copy in copies_of(b, 2 - b):
                copy.start()

    nx = st.shape[-1]
    rows = st.shape[-2]
    low_half = lax.broadcasted_iota(jnp.int32, (8, 128), 0) < HALF
    low_half_at = jnp.where(low_half, 0, 1)
    n_layers = 3 * depth

    def arrive(place):
        for copy in copies_of(place, place):
            copy.wait()
        for l in range(place * depth, (place + 1) * depth):
            for c in range(12 if second else 13):
                if sides == 2:
                    lo, hi = strips[0, c, l], strips[1, c, l]
                    left = jnp.where(low_half, hi, pltpu.roll(lo, HALF, 0))
                    right = jnp.where(low_half, pltpu.roll(hi, HALF, 0), lo)
                else:
                    v = strips[0, c, l]
                    w = pltpu.roll(v, HALF, 0)
                    keep = low_half_at == gy
                    left = jnp.where(keep, jnp.where(low_half, v, w), 0.0)
                    right = jnp.where(keep, jnp.where(low_half, w, v), 0.0)
                tile = jnp.concatenate([left, right], axis=1)
                if c == 12:
                    scale_ref[l, rows_own:rows, :] = courant * tile
                    for t in range(2):
                        pair = [strips[0, 13 + 2 * t + half, l] for half in range(2)]
                        scale_ref[l, 8 * t : 8 * t + 8, :] = courant * jnp.concatenate(pair, axis=1)
                else:
                    st[c, l, rows_own:rows, :] = tile

    row_at = lax.broadcasted_iota(jnp.int32, (rows, nx), 0)
    lane_at = lax.broadcasted_iota(jnp.int32, (rows, 128), 1)
    last_lane, first_lane = lane_at == 127, lane_at == 0
    ahead = jnp.where(info[4] > 0, courant, 0.0)
    behind = jnp.where(info[5] > 0, courant, 0.0)
    coef_in = jnp.where(row_at < rows_own, courant, jnp.where(row_at < rows_own + HALF, ahead, behind))
    low_layer, high_layer = info[2], info[3]

    def y_ahead(f):
        return pltpu.roll(f, rows - 1, 0)

    def y_behind(f):
        return pltpu.roll(f, 1, 0)

    def x_ahead(f):
        a, b = pltpu.roll(f[:, :128], 127, 1), pltpu.roll(f[:, 128:], 127, 1)
        return jnp.concatenate([jnp.where(last_lane, b, a), jnp.where(last_lane, 0.0, b)], axis=1)

    def x_behind(f):
        a, b = pltpu.roll(f[:, :128], 1, 1), pltpu.roll(f[:, 128:], 1, 1)
        return jnp.concatenate([jnp.where(first_lane, 0.0, a), jnp.where(first_lane, a, b)], axis=1)

    for m in range(1, HALF + 1):
        angle = omega_step * (m + (HALF if second else 0))
        w_re, w_im = math.cos(angle), math.sin(angle)
        for z in range(m - 1, n_layers - m):
            if m == 1 and z == 0:
                arrive(0)
            if m == 1 and (z + 1) % depth == 0:
                arrive((z + 1) // depth)
            coef = coef_in * jnp.where((z >= low_layer) & (z < high_layer), 1.0, 0.0)
            for b in (0, 6):
                ex, ey, ez = st[b, z], st[b + 1, z], st[b + 2, z]
                ex_n, ey_n = st[b, z + 1], st[b + 1, z + 1]
                st[b + 3, z] = st[b + 3, z] - coef * ((y_ahead(ez) - ez) - (ey_n - ey))
                st[b + 4, z] = st[b + 4, z] - coef * ((ex_n - ex) - (x_ahead(ez) - ez))
                if z >= m:
                    st[b + 5, z] = st[b + 5, z] - coef * ((x_ahead(ey) - ey) - (y_ahead(ex) - ex))
        for z in range(m, n_layers - m):
            scale = scale_ref[z]
            own = z - depth
            for r in range(2):
                b = 6 * r
                hx_p, hy_p = st[b + 3, z - 1], st[b + 4, z - 1]
                hx, hy, hz = st[b + 3, z], st[b + 4, z], st[b + 5, z]
                ex = st[b, z] + scale * ((hz - y_behind(hz)) - (hy - hy_p))
                ey = st[b + 1, z] + scale * ((hx - hx_p) - (hz - x_behind(hz)))
                ez = st[b + 2, z] + scale * ((hy - x_behind(hy)) - (hx - y_behind(hx)))
                for c, f in enumerate((ex, ey, ez, hx, hy, hz)):
                    if m < HALF:
                        if c < 3:
                            st[b + c, z] = f
                        continue
                    done[b + c, own] = f[:rows_own]
                    if not second:
                        up, down = f[rows_own - 8 : rows_own], f[:8]
                        if sides == 2:
                            strip_out[0][b + c, own] = strip_of(up, True)
                            strip_out[1][b + c, own] = strip_of(down, False)
                        else:
                            strip_out[0][b + c, own] = jnp.where(gy == 0, strip_of(up, True), strip_of(down, False))
                if 0 <= own < depth:
                    for c, e in enumerate((ex, ey, ez)):
                        e = e[:rows_own]
                        re, im = e * w_re, e * w_im
                        if m > 1:
                            acc[0, 3 * r + c, own] = acc[0, 3 * r + c, own] + re
                            acc[1, 3 * r + c, own] = acc[1, 3 * r + c, own] - im
                        elif second:
                            acc[0, 3 * r + c, own] = acc_in[0, 3 * r + c, own] + re
                            acc[1, 3 * r + c, own] = acc_in[1, 3 * r + c, own] - im
                        else:
                            acc[0, 3 * r + c, own] = re
                            acc[1, 3 * r + c, own] = -im

    if second:
        result = pltpu.make_async_copy(done, out, sem_out)
        result.start()
        column_sum = jnp.zeros((rows_own, nx), jnp.float32)
        for own in range(depth):
            g = jnp.zeros((rows_own, nx), jnp.float32)
            for c in range(3):
                g = g + acc[0, c, own] * acc[0, 3 + c, own] - acc[1, c, own] * acc[1, 3 + c, own]
            in_layer = (info[6] + own >= 0) & (info[6] + own < 3 * depth)
            column_sum = column_sum + jnp.where(in_layer, g, 0.0)
        sens = mm(row_table[...], mm(column_sum, col_table[...])) * (eps_span / (STEPS * 3 * depth))
        weighted = sens * slope[...]
        spectrum = mm(own_y[...], mm(weighted, basis_xt[...])) * response[...]
        shares = mm(basis_y[...], mm(spectrum, basis_x[...]))
        count, band, _ = share.shape
        n_gy = shares.shape[0] // band
        for d in range(count):
            y = d // 2 % n_gy
            share[d] = shares[y * band : (y + 1) * band]
        result.wait()


def body(fields, eps_inv, row_counts, col_counts, density):
    runs, comps, depth, rows_own, nx = fields.shape
    n_gz, n_gy = lax.axis_size("gz"), lax.axis_size("gy")
    gz, gy, core = lax.axis_index("gz"), lax.axis_index("gy"), lax.axis_index("col")
    index = gz * 2 + core
    n_z = n_gz * 2
    assert HALF == depth and rows_own == 16 and nx == 256
    rows = rows_own + 2 * HALF
    own = fields.reshape(runs * comps, depth, rows_own, nx)

    def swap_core(x):
        return lax.ppermute(x, "col", [(0, 1), (1, 0)])

    def cross(x):
        pairs = []
        for c in range(n_gz - 1):
            a, b = 2 * c + 1, 2 * c + 2
            pairs += [(a, b), (b, a)]
        return lax.ppermute(x, Z, pairs)

    if n_gy == 2:
        ways = [{0: 1, 1: 0}]
    else:
        ways = [{y: y + 1 for y in range(n_gy - 1)}, {y: y - 1 for y in range(1, n_gy)}]
    sides = len(ways)

    def along_y(x, s):
        return lax.ppermute(x, "gy", list(ways[s].items()))

    layer_start = depth * n_z // 2 - depth - depth // 2
    info = [
        core,
        gy,
        depth - index * depth,
        depth * n_z - index * depth + depth,
        jnp.where(gy < n_gy - 1, 1, 0),
        jnp.where(gy > 0, 1, 0),
        index * depth - layer_start,
    ]
    info = jnp.stack([jnp.asarray(v, jnp.int32) for v in info])

    anywhere = pl.BlockSpec(memory_space=pl.ANY)
    vmem = pl.BlockSpec(memory_space=pltpu.VMEM)
    smem = pl.BlockSpec(memory_space=pltpu.SMEM)
    shape = lambda *s: jax.ShapeDtypeStruct(s, jnp.float32)
    limit = pltpu.CompilerParams(vmem_limit_bytes=24 * 1024 * 1024)

    def strips_sent(strips, more=None):
        sent = []
        for s, strip in enumerate(strips):
            mine = along_y(strip, s)
            if more is not None and s == 0:
                mine = jnp.concatenate([mine, more])
            sent += [cross(mine), mine, swap_core(mine)]
        return sent

    starts = [(1 - gy) * (rows_own - HALF)] if sides == 1 else [rows_own - HALF, 0]
    strips = []
    for start in starts:
        rows_f = lax.dynamic_slice_in_dim(own, start, HALF, 2)
        rows_e = lax.dynamic_slice_in_dim(eps_inv, start, HALF, 1)[None]
        halves = [jnp.concatenate([f[..., :128], f[..., 128:]], 2) for f in (rows_f, rows_e)]
        strips.append(jnp.concatenate(halves))
    tiles = eps_inv.reshape(depth, 2, 8, 2, 128).transpose(1, 3, 0, 2, 4).reshape(4, depth, 8, 128)
    sent = strips_sent(strips, tiles)
    operands = [info, cross(own), own, swap_core(own)] + sent
    cost = pl.CostEstimate(flops=20_000_000, bytes_accessed=4_000_000, transcendentals=0)
    window = pltpu.VMEM((12, 3 * depth, rows, nx), jnp.float32)
    block = pltpu.VMEM((12, depth, rows_own, nx), jnp.float32)
    arrivals = [pltpu.SemaphoreType.DMA((3,)), pltpu.SemaphoreType.DMA((sides, 3))]
    state, scale, acc, *strips = pl.pallas_call(
        functools.partial(window_kernel, (depth, rows_own, sides, False)),
        out_shape=(
            shape(runs * comps, depth, rows_own, nx),
            shape(3 * depth, rows, nx),
            shape(2, 6, depth, rows_own, nx),
        )
        + (shape(12, depth, 8, 128),) * sides,
        in_specs=[smem] + [anywhere] * (3 + 3 * sides),
        out_specs=(vmem, vmem, vmem) + (vmem,) * sides,
        scratch_shapes=[
            window,
            pltpu.VMEM((sides, 17, 3 * depth, 8, 128), jnp.float32),
        ]
        + arrivals,
        compiler_params=limit,
        cost_estimate=cost,
    )(*operands)

    band, design_cols = density.shape
    tall = band * n_gy
    row_table = band_table(row_counts[0], jnp.arange(rows_own, dtype=jnp.int32)[:, None]).T
    col_table = band_table(col_counts, jnp.arange(nx, dtype=jnp.int32)[:, None])
    basis_x, wave_x = real_basis(design_cols)
    basis_y, wave_y = real_basis(tall)
    response = 1.0 / (
        1.0
        + FILTER_LEN**2
        * (
            4.0 * np.sin(math.pi * wave_y / tall)[:, None] ** 2
            + 4.0 * np.sin(math.pi * wave_x / design_cols)[None, :] ** 2
        )
    )
    const = lambda a: jnp.asarray(a, jnp.float32)
    own_y = lax.dynamic_slice_in_dim(const(basis_y), gy * band, band, 1)
    sent = strips_sent(strips)
    operands = [info, cross(state), state, swap_core(state)] + sent + [scale, acc]
    operands += [row_table, col_table, slope_of(density), const(basis_x), const(basis_x.T), const(basis_y.T), own_y, const(response)]
    n_all = n_z * n_gy
    fields_out, share = pl.pallas_call(
        functools.partial(window_kernel, (depth, rows_own, sides, True)),
        out_shape=(shape(runs * comps, depth, rows_own, nx), shape(n_all, band, design_cols)),
        in_specs=[smem] + [anywhere] * (3 + 3 * sides) + [vmem] * 10,
        out_specs=(anywhere, vmem),
        scratch_shapes=[
            window,
            pltpu.VMEM((sides, 12, 3 * depth, 8, 128), jnp.float32),
            pltpu.VMEM((2, 6, depth, rows_own, nx), jnp.float32),
            block,
        ]
        + arrivals
        + [pltpu.SemaphoreType.DMA],
        compiler_params=limit,
        cost_estimate=cost,
    )(*operands)

    got = lax.all_to_all(share, ("gz", "gy", "col"), 0, 0)
    width = design_cols // n_z
    gradient = lax.dynamic_slice_in_dim(jnp.sum(got, axis=0), index * width, width, 1)
    return fields_out.reshape(fields.shape), gradient


def solution(mesh):
    in_specs = (
        P("groups", None, ("gz", "col"), "gy", None),
        P(("groups", "gz", "col"), "gy", None),
        P(("groups", "gy"), None),
        P("groups"),
        P(("groups", "gy"), None),
    )
    out_specs = (P("groups", None, ("gz", "col"), "gy", None), P(("groups", "gy"), ("gz", "col")))
    return jax.shard_map(body, mesh=mesh, in_specs=in_specs, out_specs=out_specs, check_vma=False)
```

```python
import functools
import math

import jax
import jax.numpy as jnp
import numpy as np
from jax import lax
from jax.experimental import pallas as pl
from jax.experimental.pallas import tpu as pltpu
from jax.sharding import PartitionSpec as P

STEPS = 8
FILTER_LEN = 12

courant = 0.5
omega_step = 0.7
beta_proj = 4.0
eta_proj = 0.5
eps_span = 11.1
highest = lax.Precision.HIGHEST

Z = ("gz", "col")
HALF = STEPS // 2


def slope_of(density):
    norm = math.tanh(beta_proj * eta_proj) + math.tanh(beta_proj * (1.0 - eta_proj))
    bent = jnp.tanh(beta_proj * (density - eta_proj))
    return beta_proj * (1.0 - bent * bent) / norm


def real_basis(size):
    place = np.arange(size)
    rows, waves = [], []
    for k in range(size // 2 + 1):
        angle = 2.0 * np.pi * ((k * place) % size) / size
        edge = k == 0 or 2 * k == size
        rows.append(np.cos(angle) * math.sqrt((1.0 if edge else 2.0) / size))
        waves.append(k)
        if not edge:
            rows.append(np.sin(angle) * math.sqrt(2.0 / size))
            waves.append(k)
    return np.array(rows), np.array(waves)


def band_table(counts, place):
    ends = jnp.cumsum(counts)
    starts = ends - counts
    return ((place >= starts[None, :]) & (place < ends[None, :])).astype(jnp.float32)


def mm(left, right):
    return jnp.dot(left, right, precision=highest, preferred_element_type=jnp.float32)


def strip_of(tile, up):
    low_half = lax.broadcasted_iota(jnp.int32, (8, 128), 0) < HALF
    a, b = tile[:, :128], tile[:, 128:]
    if up:
        return jnp.where(low_half, pltpu.roll(a, HALF, 0), b)
    return jnp.where(low_half, a, pltpu.roll(b, HALF, 0))


def split(x):
    high = x.astype(jnp.bfloat16).astype(jnp.float32)
    return high, x - high


def mix(table, x, start=0):
    total = table[start] * x[:1]
    for k in range(1, x.shape[0]):
        total = total + table[start + k] * x[k : k + 1]
    return total


def placed(x, at, size):
    rows = x.shape[0]
    block = lax.broadcasted_iota(jnp.int32, (size, x.shape[1]), 0) // rows
    return jnp.where(block == at, jnp.concatenate([x] * (size // rows)), 0.0)


def transform(x, basis):
    rows, columns = x.shape
    parts = jnp.concatenate(split(x)).astype(jnp.bfloat16)
    product = jnp.dot(parts, basis[...].astype(jnp.bfloat16), preferred_element_type=jnp.float32)
    small = product[rows:, :columns] + product[:rows, columns:] + product[rows:, columns:]
    return product[:rows, :columns] + small


def window_kernel(cfg, *refs):
    depth, rows_own, sides, second = cfg
    it = iter(refs)
    take = lambda n: [next(it) for _ in range(n)]
    info = next(it)
    pieces = 2 if second else 1
    full = [take(3) for _ in range(pieces)]
    strip_in = [take(3) for _ in range(sides)]
    if second:
        (scale_ref, acc_in) = take(2)
        row_wide, col_table, slope, basis_x, basis_xt, basis_y, basis_yt, response = take(8)
        out, share = take(2)
        st, strips, acc, done, sem_full, sem_strip, sem_out = take(7)
    else:
        done = take(2)
        scale_ref, acc = take(2)
        strip_out = take(sides)
        st, strips, sem_full, sem_strip = take(4)

    core, gy = info[0], info[1]

    def copies_of(b, place):
        layers = pl.ds(place * depth, depth)
        found = []
        for p in range(pieces):
            planes = pl.ds(12 // pieces * p, 12 // pieces)
            found.append(
                pltpu.make_async_copy(
                    full[p][b], st.at[planes, layers, pl.ds(0, rows_own), :], sem_full.at[p, place]
                )
            )
        for s in range(sides):
            planes = pl.ds(0, strip_in[s][b].shape[0])
            found.append(pltpu.make_async_copy(strip_in[s][b], strips.at[s, planes, layers], sem_strip.at[s, place]))
        return found

    @pl.when(core == 0)
    def _():
        for b in range(3):
            for copy in copies_of(b, b):
                copy.start()

    @pl.when(core != 0)
    def _():
        for b in (2, 1, 0):
            for copy in copies_of(b, 2 - b):
                copy.start()

    nx = st.shape[-1]
    rows = st.shape[-2]
    low_half = lax.broadcasted_iota(jnp.int32, (8, 128), 0) < HALF
    low_half_at = jnp.where(low_half, 0, 1)
    n_layers = 3 * depth

    def arrive(place):
        for copy in copies_of(place, place):
            copy.wait()
        for l in range(place * depth, (place + 1) * depth):
            for c in range(12 if second else 13):
                if sides == 2:
                    lo, hi = strips[0, c, l], strips[1, c, l]
                    left = jnp.where(low_half, hi, pltpu.roll(lo, HALF, 0))
                    right = jnp.where(low_half, pltpu.roll(hi, HALF, 0), lo)
                else:
                    v = strips[0, c, l]
                    w = pltpu.roll(v, HALF, 0)
                    keep = low_half_at == gy
                    left = jnp.where(keep, jnp.where(low_half, v, w), 0.0)
                    right = jnp.where(keep, jnp.where(low_half, w, v), 0.0)
                tile = jnp.concatenate([left, right], axis=1)
                if c == 12:
                    scale_ref[l, rows_own:rows, :] = courant * tile
                    for t in range(2):
                        pair = [strips[0, 13 + 2 * t + half, l] for half in range(2)]
                        scale_ref[l, 8 * t : 8 * t + 8, :] = courant * jnp.concatenate(pair, axis=1)
                else:
                    st[c, l, rows_own:rows, :] = tile

    row_at = lax.broadcasted_iota(jnp.int32, (rows, nx), 0)
    lane_at = lax.broadcasted_iota(jnp.int32, (rows, 128), 1)
    last_lane, first_lane = lane_at == 127, lane_at == 0
    ahead = jnp.where(info[4] > 0, courant, 0.0)
    behind = jnp.where(info[5] > 0, courant, 0.0)
    coef_in = jnp.where(row_at < rows_own, courant, jnp.where(row_at < rows_own + HALF, ahead, behind))
    low_layer, high_layer = info[2], info[3]

    def y_ahead(f):
        return pltpu.roll(f, rows - 1, 0)

    def y_behind(f):
        return pltpu.roll(f, 1, 0)

    def x_ahead(f):
        a, b = pltpu.roll(f[:, :128], 127, 1), pltpu.roll(f[:, 128:], 127, 1)
        return jnp.concatenate([jnp.where(last_lane, b, a), jnp.where(last_lane, 0.0, b)], axis=1)

    def x_behind(f):
        a, b = pltpu.roll(f[:, :128], 1, 1), pltpu.roll(f[:, 128:], 1, 1)
        return jnp.concatenate([jnp.where(first_lane, 0.0, a), jnp.where(first_lane, a, b)], axis=1)

    for m in range(1, HALF + 1):
        angle = omega_step * (m + (HALF if second else 0))
        w_re, w_im = math.cos(angle), math.sin(angle)
        for z in range(m - 1, n_layers - m):
            if m == 1 and z == 0:
                arrive(0)
            if m == 1 and (z + 1) % depth == 0:
                arrive((z + 1) // depth)
            coef = coef_in * jnp.where((z >= low_layer) & (z < high_layer), 1.0, 0.0)
            for b in (0, 6):
                ex, ey, ez = st[b, z], st[b + 1, z], st[b + 2, z]
                ex_n, ey_n = st[b, z + 1], st[b + 1, z + 1]
                st[b + 3, z] = st[b + 3, z] - coef * ((y_ahead(ez) - ez) - (ey_n - ey))
                st[b + 4, z] = st[b + 4, z] - coef * ((ex_n - ex) - (x_ahead(ez) - ez))
                if z >= m:
                    st[b + 5, z] = st[b + 5, z] - coef * ((x_ahead(ey) - ey) - (y_ahead(ex) - ex))
        for z in range(m, n_layers - m):
            scale = scale_ref[z]
            own = z - depth
            for r in range(2):
                b = 6 * r
                hx_p, hy_p = st[b + 3, z - 1], st[b + 4, z - 1]
                hx, hy, hz = st[b + 3, z], st[b + 4, z], st[b + 5, z]
                ex = st[b, z] + scale * ((hz - y_behind(hz)) - (hy - hy_p))
                ey = st[b + 1, z] + scale * ((hx - hx_p) - (hz - x_behind(hz)))
                ez = st[b + 2, z] + scale * ((hy - x_behind(hy)) - (hx - y_behind(hx)))
                for c, f in enumerate((ex, ey, ez, hx, hy, hz)):
                    if m < HALF:
                        if c < 3:
                            st[b + c, z] = f
                        continue
                    if second:
                        done[b + c, own] = f[:rows_own]
                    else:
                        done[r][c, own] = f[:rows_own]
                        up, down = f[rows_own - 8 : rows_own], f[:8]
                        if sides == 2:
                            strip_out[0][b + c, own] = strip_of(up, True)
                            strip_out[1][b + c, own] = strip_of(down, False)
                        else:
                            strip_out[0][b + c, own] = jnp.where(gy == 0, strip_of(up, True), strip_of(down, False))
                if 0 <= own < depth:
                    for c, e in enumerate((ex, ey, ez)):
                        e = e[:rows_own]
                        re, im = e * w_re, e * w_im
                        if m > 1:
                            acc[0, 3 * r + c, own] = acc[0, 3 * r + c, own] + re
                            acc[1, 3 * r + c, own] = acc[1, 3 * r + c, own] - im
                        elif second:
                            acc[0, 3 * r + c, own] = acc_in[0, 3 * r + c, own] + re
                            acc[1, 3 * r + c, own] = acc_in[1, 3 * r + c, own] - im
                        else:
                            acc[0, 3 * r + c, own] = re
                            acc[1, 3 * r + c, own] = -im

    if second:
        result = pltpu.make_async_copy(done, out, sem_out)
        result.start()
        column_sum = jnp.zeros((rows_own, nx), jnp.float32)
        for own in range(depth):
            g = jnp.zeros((rows_own, nx), jnp.float32)
            for c in range(3):
                g = g + acc[0, c, own] * acc[0, 3 + c, own] - acc[1, c, own] * acc[1, 3 + c, own]
            in_layer = (info[6] + own >= 0) & (info[6] + own < 3 * depth)
            column_sum = column_sum + jnp.where(in_layer, g, 0.0)
        pooled = jnp.zeros(row_wide.shape[1:], jnp.float32)
        for k in range(rows_own):
            pooled = pooled + row_wide[k] * column_sum[k : k + 1]
        high, rest = split(pooled)
        mid, low = split(rest)
        parts = jnp.concatenate([high, mid, low, jnp.zeros_like(low)]).astype(jnp.bfloat16)
        parts = jnp.dot(parts, col_table[...].astype(jnp.bfloat16), preferred_element_type=jnp.float32)
        band = pooled.shape[0]
        sens = (parts[:band] + parts[band : 2 * band] + parts[2 * band : 3 * band]) * (eps_span / (STEPS * 3 * depth))
        weighted = sens * slope[...]
        tall = response.shape[0]
        if len(basis_y.shape) == 3:
            spectrum = transform(mix(basis_yt, weighted, gy * band), basis_xt) * response[...]
            shares = mix(basis_y, transform(spectrum, basis_x))
        else:
            spectrum = transform(mm(basis_y[...], placed(weighted, gy, tall)), basis_xt) * response[...]
            shares = mm(basis_yt[...], transform(spectrum, basis_x))
        count = share.shape[0]
        n_gy = shares.shape[0] // band
        for d in range(count):
            y = d // 2 % n_gy
            share[d] = shares[y * band : (y + 1) * band]
        result.wait()


def body(fields, eps_inv, row_counts, col_counts, density):
    runs, comps, depth, rows_own, nx = fields.shape
    n_gz, n_gy = lax.axis_size("gz"), lax.axis_size("gy")
    gz, gy, core = lax.axis_index("gz"), lax.axis_index("gy"), lax.axis_index("col")
    index = gz * 2 + core
    n_z = n_gz * 2
    assert HALF == depth and rows_own == 16 and nx == 256
    rows = rows_own + 2 * HALF
    own = fields.reshape(runs * comps, depth, rows_own, nx)

    def swap_core(x):
        return lax.ppermute(x, "col", [(0, 1), (1, 0)])

    def cross(x):
        pairs = []
        for c in range(n_gz - 1):
            a, b = 2 * c + 1, 2 * c + 2
            pairs += [(a, b), (b, a)]
        return lax.ppermute(x, Z, pairs)

    if n_gy == 2:
        ways = [{0: 1, 1: 0}]
    else:
        ways = [{y: y + 1 for y in range(n_gy - 1)}, {y: y - 1 for y in range(1, n_gy)}]
    sides = len(ways)

    def along_y(x, s):
        return lax.ppermute(x, "gy", list(ways[s].items()))

    layer_start = depth * n_z // 2 - depth - depth // 2
    info = [
        core,
        gy,
        depth - index * depth,
        depth * n_z - index * depth + depth,
        jnp.where(gy < n_gy - 1, 1, 0),
        jnp.where(gy > 0, 1, 0),
        index * depth - layer_start,
    ]
    info = jnp.stack([jnp.asarray(v, jnp.int32) for v in info])

    anywhere = pl.BlockSpec(memory_space=pl.ANY)
    vmem = pl.BlockSpec(memory_space=pltpu.VMEM)
    smem = pl.BlockSpec(memory_space=pltpu.SMEM)
    shape = lambda *s: jax.ShapeDtypeStruct(s, jnp.float32)
    limit = pltpu.CompilerParams(vmem_limit_bytes=24 * 1024 * 1024)

    def strips_sent(strips, more=None):
        sent = []
        for s, strip in enumerate(strips):
            mine = along_y(strip, s)
            if more is not None and s == 0:
                mine = jnp.concatenate([mine, more])
            sent += [cross(mine), mine, swap_core(mine)]
        return sent

    starts = [(1 - gy) * (rows_own - HALF)] if sides == 1 else [rows_own - HALF, 0]
    strips = []
    for start in starts:
        rows_f = lax.dynamic_slice_in_dim(own, start, HALF, 2)
        rows_e = lax.dynamic_slice_in_dim(eps_inv, start, HALF, 1)[None]
        halves = [jnp.concatenate([f[..., :128], f[..., 128:]], 2) for f in (rows_f, rows_e)]
        strips.append(jnp.concatenate(halves))
    tiles = eps_inv.reshape(depth, 2, 8, 2, 128).transpose(1, 3, 0, 2, 4).reshape(4, depth, 8, 128)
    sent = strips_sent(strips, tiles)
    operands = [info, cross(own), own, swap_core(own)] + sent
    cost = pl.CostEstimate(flops=20_000_000, bytes_accessed=4_000_000, transcendentals=0)
    window = pltpu.VMEM((12, 3 * depth, rows, nx), jnp.float32)
    block = pltpu.VMEM((12, depth, rows_own, nx), jnp.float32)
    arrivals = [pltpu.SemaphoreType.DMA((2, 3)), pltpu.SemaphoreType.DMA((sides, 3))]
    half_0, half_1, scale, acc, *strips = pl.pallas_call(
        functools.partial(window_kernel, (depth, rows_own, sides, False)),
        out_shape=(
            shape(comps, depth, rows_own, nx),
            shape(comps, depth, rows_own, nx),
            shape(3 * depth, rows, nx),
            shape(2, 6, depth, rows_own, nx),
        )
        + (shape(12, depth, 8, 128),) * sides,
        in_specs=[smem] + [anywhere] * (3 + 3 * sides),
        out_specs=(vmem,) * (4 + sides),
        scratch_shapes=[
            window,
            pltpu.VMEM((sides, 17, 3 * depth, 8, 128), jnp.float32),
        ]
        + arrivals,
        compiler_params=limit,
        cost_estimate=cost,
    )(*operands)

    band, design_cols = density.shape
    tall = band * n_gy
    row_table = band_table(row_counts[0], jnp.arange(rows_own, dtype=jnp.int32)[:, None])
    row_wide = jnp.broadcast_to(row_table[:, :, None], (rows_own, band, nx))
    col_table = band_table(col_counts, jnp.arange(nx, dtype=jnp.int32)[:, None])
    basis_x, wave_x = real_basis(design_cols)
    basis_y, wave_y = real_basis(tall)
    response = 1.0 / (
        1.0
        + FILTER_LEN**2
        * (
            4.0 * np.sin(math.pi * wave_y / tall)[:, None] ** 2
            + 4.0 * np.sin(math.pi * wave_x / design_cols)[None, :] ** 2
        )
    )
    const = lambda a: jnp.asarray(a, jnp.float32)
    tables = [basis_y, basis_y.T]
    if tall <= 16:
        tables = [np.broadcast_to(t[:, :, None], (tall, tall, design_cols)) for t in tables]

    def halves(matrix):
        high = matrix.astype(jnp.bfloat16).astype(np.float64)
        return const(np.concatenate([high, matrix - high], axis=1))

    sent = strips_sent(strips)
    operands = [info]
    for half in (half_0, half_1):
        operands += [cross(half), half, swap_core(half)]
    operands += sent + [scale, acc]
    operands += [row_wide, col_table, slope_of(density), halves(basis_x), halves(basis_x.T)]
    operands += [const(tables[0]), const(tables[1]), const(response)]
    n_all = n_z * n_gy
    fields_out, share = pl.pallas_call(
        functools.partial(window_kernel, (depth, rows_own, sides, True)),
        out_shape=(shape(runs * comps, depth, rows_own, nx), shape(n_all, band, design_cols)),
        in_specs=[smem] + [anywhere] * (6 + 3 * sides) + [vmem] * 10,
        out_specs=(anywhere, vmem),
        scratch_shapes=[
            window,
            pltpu.VMEM((sides, 12, 3 * depth, 8, 128), jnp.float32),
            pltpu.VMEM((2, 6, depth, rows_own, nx), jnp.float32),
            block,
        ]
        + arrivals
        + [pltpu.SemaphoreType.DMA],
        compiler_params=limit,
        cost_estimate=cost,
    )(*operands)

    got = lax.all_to_all(share, ("gz", "gy", "col"), 0, 0)
    width = design_cols // n_z
    gradient = lax.dynamic_slice_in_dim(jnp.sum(got, axis=0), index * width, width, 1)
    return fields_out.reshape(fields.shape), gradient


def solution(mesh):
    in_specs = (
        P("groups", None, ("gz", "col"), "gy", None),
        P(("groups", "gz", "col"), "gy", None),
        P(("groups", "gy"), None),
        P("groups"),
        P(("groups", "gy"), None),
    )
    out_specs = (P("groups", None, ("gz", "col"), "gy", None), P(("groups", "gy"), ("gz", "col")))
    return jax.shard_map(body, mesh=mesh, in_specs=in_specs, out_specs=out_specs, check_vma=False)
```

```python
import functools
import math

import jax
import jax.numpy as jnp
import numpy as np
from jax import lax
from jax.experimental import pallas as pl
from jax.experimental.pallas import tpu as pltpu
from jax.sharding import PartitionSpec as P

STEPS = 8
FILTER_LEN = 12

courant = 0.5
omega_step = 0.7
beta_proj = 4.0
eta_proj = 0.5
eps_span = 11.1
highest = lax.Precision.HIGHEST

Z = ("gz", "col")
HALF = STEPS // 2


def slope_of(density):
    norm = math.tanh(beta_proj * eta_proj) + math.tanh(beta_proj * (1.0 - eta_proj))
    bent = jnp.tanh(beta_proj * (density - eta_proj))
    return beta_proj * (1.0 - bent * bent) / norm


def real_basis(size):
    place = np.arange(size)
    rows, waves = [], []
    for k in range(size // 2 + 1):
        angle = 2.0 * np.pi * ((k * place) % size) / size
        edge = k == 0 or 2 * k == size
        rows.append(np.cos(angle) * math.sqrt((1.0 if edge else 2.0) / size))
        waves.append(k)
        if not edge:
            rows.append(np.sin(angle) * math.sqrt(2.0 / size))
            waves.append(k)
    return np.array(rows), np.array(waves)


def mm(left, right):
    return jnp.dot(left, right, precision=highest, preferred_element_type=jnp.float32)


def strip_of(tile, up):
    low_half = lax.broadcasted_iota(jnp.int32, (8, 128), 0) < HALF
    a, b = tile[:, :128], tile[:, 128:]
    if up:
        return jnp.where(low_half, pltpu.roll(a, HALF, 0), b)
    return jnp.where(low_half, a, pltpu.roll(b, HALF, 0))


def split(x):
    high = x.astype(jnp.bfloat16).astype(jnp.float32)
    return high, x - high


def mix(table, x, start=0):
    total = table[start] * x[:1]
    for k in range(1, x.shape[0]):
        total = total + table[start + k] * x[k : k + 1]
    return total


def placed(x, at, size):
    rows = x.shape[0]
    block = lax.broadcasted_iota(jnp.int32, (size, x.shape[1]), 0) // rows
    return jnp.where(block == at, jnp.concatenate([x] * (size // rows)), 0.0)


def transform(x, basis):
    rows, columns = x.shape
    parts = jnp.concatenate(split(x)).astype(jnp.bfloat16)
    product = jnp.dot(parts, basis[...].astype(jnp.bfloat16), preferred_element_type=jnp.float32)
    small = product[rows:, :columns] + product[:rows, columns:] + product[rows:, columns:]
    return product[:rows, :columns] + small


def window_kernel(cfg, *refs):
    depth, rows_own, sides, second = cfg
    it = iter(refs)
    take = lambda n: [next(it) for _ in range(n)]
    n_z, n_gy = 2 * lax.axis_size("gz"), lax.axis_size("gy")
    core, gy = lax.axis_index("col"), lax.axis_index("gy")
    first_layer = (2 * lax.axis_index("gz") + core) * depth
    layer_start = depth * n_z // 2 - depth - depth // 2
    pieces = 2 if second else 1
    full = [take(pieces), take(1), take(1)]
    strip_in = [take(3) for _ in range(sides)]
    if second:
        (scale_ref, acc_in) = take(2)
        row_wide, col_table, slope, basis_x, basis_xt, basis_y, basis_yt, response = take(8)
        out, share = take(2)
        st, strips, acc, done, sem_full, sem_strip, sem_out = take(7)
    else:
        done = take(3)
        scale_ref, acc = take(2)
        strip_out = take(sides)
        st, strips, eps, sem_full, sem_strip, sem_eps = take(6)

    def copies_of(b, place):
        layers = pl.ds(place * depth, depth)
        found = []
        for p, ref in enumerate(full[b]):
            count = min(ref.shape[0], 12)
            planes = pl.ds(count * p, count)
            found.append(
                pltpu.make_async_copy(
                    ref.at[pl.ds(0, count)], st.at[planes, layers, pl.ds(0, rows_own), :], sem_full.at[p, place]
                )
            )
        for s in range(sides):
            found.append(pltpu.make_async_copy(strip_in[s][b], strips.at[s, :, layers], sem_strip.at[s, place]))
        if not second:
            found.append(pltpu.make_async_copy(full[b][0].at[12], eps.at[layers], sem_eps.at[place]))
        return found

    @pl.when(core == 0)
    def _():
        for b in range(3):
            for copy in copies_of(b, b):
                copy.start()

    @pl.when(core != 0)
    def _():
        for b in (2, 1, 0):
            for copy in copies_of(b, 2 - b):
                copy.start()

    nx = st.shape[-1]
    rows = st.shape[-2]
    low_half = lax.broadcasted_iota(jnp.int32, (8, 128), 0) < HALF
    low_half_at = jnp.where(low_half, 0, 1)
    n_layers = 3 * depth

    def arrive(place):
        if place == 1:
            for copy in copies_of(1, 1):
                copy.wait()
        else:
            here = core == place // 2

            @pl.when(here)
            def _():
                for copy in copies_of(0, place):
                    copy.wait()

            @pl.when(jnp.logical_not(here))
            def _():
                for copy in copies_of(2, place):
                    copy.wait()

        for l in range(place * depth, (place + 1) * depth):
            for c in range(12 if second else 13):
                if sides == 2:
                    lo, hi = strips[0, c, l], strips[1, c, l]
                    left = jnp.where(low_half, hi, pltpu.roll(lo, HALF, 0))
                    right = jnp.where(low_half, pltpu.roll(hi, HALF, 0), lo)
                else:
                    v = strips[0, c, l]
                    w = pltpu.roll(v, HALF, 0)
                    keep = low_half_at == gy
                    left = jnp.where(keep, jnp.where(low_half, v, w), 0.0)
                    right = jnp.where(keep, jnp.where(low_half, w, v), 0.0)
                tile = jnp.concatenate([left, right], axis=1)
                if c == 12:
                    scale_ref[l, rows_own:rows, :] = courant * tile
                    scale_ref[l, :rows_own, :] = courant * eps[l]
                else:
                    st[c, l, rows_own:rows, :] = tile

    row_at = lax.broadcasted_iota(jnp.int32, (rows, nx), 0)
    lane_at = lax.broadcasted_iota(jnp.int32, (rows, 128), 1)
    last_lane, first_lane = lane_at == 127, lane_at == 0
    ahead = jnp.where(gy < n_gy - 1, courant, 0.0)
    behind = jnp.where(gy > 0, courant, 0.0)
    coef_in = jnp.where(row_at < rows_own, courant, jnp.where(row_at < rows_own + HALF, ahead, behind))
    low_layer = depth - first_layer
    high_layer = low_layer + depth * n_z

    def y_ahead(f):
        return pltpu.roll(f, rows - 1, 0)

    def y_behind(f):
        return pltpu.roll(f, 1, 0)

    def x_ahead(f):
        a, b = pltpu.roll(f[:, :128], 127, 1), pltpu.roll(f[:, 128:], 127, 1)
        return jnp.concatenate([jnp.where(last_lane, b, a), jnp.where(last_lane, 0.0, b)], axis=1)

    def x_behind(f):
        a, b = pltpu.roll(f[:, :128], 1, 1), pltpu.roll(f[:, 128:], 1, 1)
        return jnp.concatenate([jnp.where(first_lane, 0.0, a), jnp.where(first_lane, a, b)], axis=1)

    for m in range(1, HALF + 1):
        angle = omega_step * (m + (HALF if second else 0))
        w_re, w_im = math.cos(angle), math.sin(angle)
        for z in range(m - 1, n_layers - m):
            if m == 1 and z == 0:
                arrive(0)
            if m == 1 and (z + 1) % depth == 0:
                arrive((z + 1) // depth)
            coef = coef_in * jnp.where((z >= low_layer) & (z < high_layer), 1.0, 0.0)
            for b in (0, 6):
                ex, ey, ez = st[b, z], st[b + 1, z], st[b + 2, z]
                ex_n, ey_n = st[b, z + 1], st[b + 1, z + 1]
                st[b + 3, z] = st[b + 3, z] - coef * ((y_ahead(ez) - ez) - (ey_n - ey))
                st[b + 4, z] = st[b + 4, z] - coef * ((ex_n - ex) - (x_ahead(ez) - ez))
                if z >= m:
                    st[b + 5, z] = st[b + 5, z] - coef * ((x_ahead(ey) - ey) - (y_ahead(ex) - ex))
        for z in range(m, n_layers - m):
            scale = scale_ref[z]
            own = z - depth
            for r in range(2):
                b = 6 * r
                hx_p, hy_p = st[b + 3, z - 1], st[b + 4, z - 1]
                hx, hy, hz = st[b + 3, z], st[b + 4, z], st[b + 5, z]
                ex = st[b, z] + scale * ((hz - y_behind(hz)) - (hy - hy_p))
                ey = st[b + 1, z] + scale * ((hx - hx_p) - (hz - x_behind(hz)))
                ez = st[b + 2, z] + scale * ((hy - x_behind(hy)) - (hx - y_behind(hx)))
                for c, f in enumerate((ex, ey, ez, hx, hy, hz)):
                    if m < HALF:
                        if c < 3:
                            st[b + c, z] = f
                        continue
                    if second:
                        done[b + c, own] = f[:rows_own]
                    else:
                        done[r][c, own] = f[:rows_own]
                        done[2][b + c, own] = f[:rows_own]
                        up, down = f[rows_own - 8 : rows_own], f[:8]
                        if sides == 2:
                            strip_out[0][b + c, own] = strip_of(up, True)
                            strip_out[1][b + c, own] = strip_of(down, False)
                        else:
                            strip_out[0][b + c, own] = jnp.where(gy == 0, strip_of(up, True), strip_of(down, False))
                if 0 <= own < depth:
                    for c, e in enumerate((ex, ey, ez)):
                        e = e[:rows_own]
                        re, im = e * w_re, e * w_im
                        if m > 1:
                            acc[0, 3 * r + c, own] = acc[0, 3 * r + c, own] + re
                            acc[1, 3 * r + c, own] = acc[1, 3 * r + c, own] - im
                        elif second:
                            acc[0, 3 * r + c, own] = acc_in[0, 3 * r + c, own] + re
                            acc[1, 3 * r + c, own] = acc_in[1, 3 * r + c, own] - im
                        else:
                            acc[0, 3 * r + c, own] = re
                            acc[1, 3 * r + c, own] = -im

    if second:
        result = pltpu.make_async_copy(done, out, sem_out)
        result.start()
        column_sum = jnp.zeros((rows_own, nx), jnp.float32)
        for own in range(depth):
            g = jnp.zeros((rows_own, nx), jnp.float32)
            for c in range(3):
                g = g + acc[0, c, own] * acc[0, 3 + c, own] - acc[1, c, own] * acc[1, 3 + c, own]
            layer = first_layer + own - layer_start
            in_layer = (layer >= 0) & (layer < 3 * depth)
            column_sum = column_sum + jnp.where(in_layer, g, 0.0)
        pooled = jnp.zeros(row_wide.shape[1:], jnp.float32)
        for k in range(rows_own):
            pooled = pooled + row_wide[k] * column_sum[k : k + 1]
        high, rest = split(pooled)
        mid, low = split(rest)
        parts = jnp.concatenate([high, mid, low, jnp.zeros_like(low)]).astype(jnp.bfloat16)
        parts = jnp.dot(parts, col_table[...].astype(jnp.bfloat16), preferred_element_type=jnp.float32)
        band = pooled.shape[0]
        sens = (parts[:band] + parts[band : 2 * band] + parts[2 * band : 3 * band]) * (eps_span / (STEPS * 3 * depth))
        weighted = sens * slope[...]
        tall = response.shape[0]
        if len(basis_y.shape) == 3:
            spectrum = transform(mix(basis_yt, weighted, gy * band), basis_xt) * response[...]
            shares = mix(basis_y, transform(spectrum, basis_x))
        else:
            spectrum = transform(mm(basis_y[...], placed(weighted, gy, tall)), basis_xt) * response[...]
            shares = mm(basis_yt[...], transform(spectrum, basis_x))
        count = share.shape[0]
        for d in range(count):
            y = d // 2 % n_gy
            share[d] = shares[y * band : (y + 1) * band]
        result.wait()


def table_kernel(row_counts, col_counts, row_wide, col_table):
    band, nx = row_wide.shape[1:]
    row = lax.broadcasted_iota(jnp.int32, (band, nx), 0)
    start = jnp.zeros((band, nx), jnp.int32)
    stop = jnp.zeros((band, nx), jnp.int32)
    total = jnp.int32(0)
    for k in range(band):
        start = jnp.where(row == k, total, start)
        total = total + row_counts[0, k]
        stop = jnp.where(row == k, total, stop)
    for p in range(row_wide.shape[0]):
        row_wide[p] = jnp.where((start <= p) & (p < stop), 1.0, 0.0)
    width = col_table.shape[1]
    counts = jnp.broadcast_to(col_counts[...].astype(jnp.float32), (16, width))
    before = lax.broadcasted_iota(jnp.int32, (width, width), 0) <= lax.broadcasted_iota(jnp.int32, (width, width), 1)
    upto = jnp.where(before, 1.0, 0.0).astype(jnp.bfloat16)
    ends = jnp.dot(counts.astype(jnp.bfloat16), upto, preferred_element_type=jnp.float32)
    starts = ends - counts
    place = lax.broadcasted_iota(jnp.int32, col_table.shape, 0).astype(jnp.float32)
    col_table[...] = jnp.where((place >= starts[:1]) & (place < ends[:1]), 1.0, 0.0)


def body(fields, eps_inv, row_counts, col_counts, density):
    runs, comps, depth, rows_own, nx = fields.shape
    n_gz, n_gy = lax.axis_size("gz"), lax.axis_size("gy")
    gz, gy, core = lax.axis_index("gz"), lax.axis_index("gy"), lax.axis_index("col")
    index = gz * 2 + core
    n_z = n_gz * 2
    assert HALF == depth and rows_own == 16 and nx == 256
    rows = rows_own + 2 * HALF
    own = jnp.concatenate([fields.reshape(runs * comps, depth, rows_own, nx), eps_inv[None]])

    def swap_core(x):
        return lax.ppermute(x, "col", [(0, 1), (1, 0)])

    def cross(x):
        pairs = []
        for c in range(n_gz - 1):
            a, b = 2 * c + 1, 2 * c + 2
            pairs += [(a, b), (b, a)]
        return lax.ppermute(x, Z, pairs)

    if n_gy == 2:
        ways = [{0: 1, 1: 0}]
    else:
        ways = [{y: y + 1 for y in range(n_gy - 1)}, {y: y - 1 for y in range(1, n_gy)}]
    sides = len(ways)

    def along_y(x, s):
        return lax.ppermute(x, "gy", list(ways[s].items()))

    anywhere = pl.BlockSpec(memory_space=pl.ANY)
    vmem = pl.BlockSpec(memory_space=pltpu.VMEM)
    smem = pl.BlockSpec(memory_space=pltpu.SMEM)
    shape = lambda *s: jax.ShapeDtypeStruct(s, jnp.float32)
    limit = pltpu.CompilerParams(vmem_limit_bytes=24 * 1024 * 1024)

    def strips_sent(strips):
        sent = []
        for s, strip in enumerate(strips):
            mine = along_y(strip, s)
            far = cross(mine)
            sent += [far, mine, swap_core(mine)]
        return sent

    starts = [(1 - gy) * (rows_own - HALF)] if sides == 1 else [rows_own - HALF, 0]
    strips = []
    for start in starts:
        edge = lax.dynamic_slice_in_dim(own, start, HALF, 2)
        strips.append(jnp.concatenate([edge[..., :128], edge[..., 128:]], 2))
    sent = strips_sent(strips)
    operands = [cross(own), own, swap_core(own)] + sent
    cost = pl.CostEstimate(flops=20_000_000, bytes_accessed=4_000_000, transcendentals=0)
    window = pltpu.VMEM((12, 3 * depth, rows, nx), jnp.float32)
    block = pltpu.VMEM((12, depth, rows_own, nx), jnp.float32)
    arrivals = [pltpu.SemaphoreType.DMA((2, 3)), pltpu.SemaphoreType.DMA((sides, 3))]
    half_0, half_1, state, scale, acc, *strips = pl.pallas_call(
        functools.partial(window_kernel, (depth, rows_own, sides, False)),
        out_shape=(
            shape(comps, depth, rows_own, nx),
            shape(comps, depth, rows_own, nx),
            shape(runs * comps, depth, rows_own, nx),
            shape(3 * depth, rows, nx),
            shape(2, 6, depth, rows_own, nx),
        )
        + (shape(12, depth, 8, 128),) * sides,
        in_specs=[anywhere] * (3 + 3 * sides),
        out_specs=(vmem,) * (5 + sides),
        scratch_shapes=[
            window,
            pltpu.VMEM((sides, 13, 3 * depth, 8, 128), jnp.float32),
            pltpu.VMEM((3 * depth, rows_own, nx), jnp.float32),
        ]
        + arrivals
        + [pltpu.SemaphoreType.DMA((3,))],
        compiler_params=limit,
        cost_estimate=cost,
    )(*operands)

    band, design_cols = density.shape
    tall = band * n_gy
    row_wide, col_table = pl.pallas_call(
        table_kernel,
        out_shape=(shape(rows_own, band, nx), shape(nx, design_cols)),
        in_specs=[smem, vmem],
        out_specs=(vmem, vmem),
        compiler_params=pltpu.CompilerParams(vmem_limit_bytes=4 * 1024 * 1024),
    )(row_counts, col_counts.reshape(1, design_cols))
    basis_x, wave_x = real_basis(design_cols)
    basis_y, wave_y = real_basis(tall)
    response = 1.0 / (
        1.0
        + FILTER_LEN**2
        * (
            4.0 * np.sin(math.pi * wave_y / tall)[:, None] ** 2
            + 4.0 * np.sin(math.pi * wave_x / design_cols)[None, :] ** 2
        )
    )
    const = lambda a: jnp.asarray(a, jnp.float32)
    tables = [basis_y, basis_y.T]
    if tall <= 16:
        tables = [np.broadcast_to(t[:, :, None], (tall, tall, design_cols)) for t in tables]

    def halves(matrix):
        high = matrix.astype(jnp.bfloat16).astype(np.float64)
        return const(np.concatenate([high, matrix - high], axis=1))

    sent = strips_sent(strips)
    operands = [cross(half_0), cross(half_1), state, swap_core(state)]
    operands += sent + [scale, acc]
    operands += [row_wide, col_table, slope_of(density), halves(basis_x), halves(basis_x.T)]
    operands += [const(tables[0]), const(tables[1]), const(response)]
    n_all = n_z * n_gy
    fields_out, share = pl.pallas_call(
        functools.partial(window_kernel, (depth, rows_own, sides, True)),
        out_shape=(shape(runs * comps, depth, rows_own, nx), shape(n_all, band, design_cols)),
        in_specs=[anywhere] * (4 + 3 * sides) + [vmem] * 10,
        out_specs=(anywhere, vmem),
        scratch_shapes=[
            window,
            pltpu.VMEM((sides, 12, 3 * depth, 8, 128), jnp.float32),
            pltpu.VMEM((2, 6, depth, rows_own, nx), jnp.float32),
            block,
        ]
        + arrivals
        + [pltpu.SemaphoreType.DMA],
        compiler_params=limit,
        cost_estimate=cost,
    )(*operands)

    got = lax.all_to_all(share, ("gz", "gy", "col"), 0, 0)
    width = design_cols // n_z
    gradient = lax.dynamic_slice_in_dim(jnp.sum(got, axis=0), index * width, width, 1)
    return fields_out.reshape(fields.shape), gradient


def solution(mesh):
    in_specs = (
        P("groups", None, ("gz", "col"), "gy", None),
        P(("groups", "gz", "col"), "gy", None),
        P(("groups", "gy"), None),
        P("groups"),
        P(("groups", "gy"), None),
    )
    out_specs = (P("groups", None, ("gz", "col"), "gy", None), P(("groups", "gy"), ("gz", "col")))
    return jax.shard_map(body, mesh=mesh, in_specs=in_specs, out_specs=out_specs, check_vma=False)
```

```python
import functools
import math

import jax
import jax.numpy as jnp
import numpy as np
from jax import lax
from jax.experimental import pallas as pl
from jax.experimental.pallas import tpu as pltpu
from jax.sharding import PartitionSpec as P

STEPS = 8
FILTER_LEN = 12

courant = 0.5
omega_step = 0.7
beta_proj = 4.0
eta_proj = 0.5
eps_span = 11.1
highest = lax.Precision.HIGHEST

Z = ("gz", "col")
HALF = STEPS // 2


def slope_of(density):
    norm = math.tanh(beta_proj * eta_proj) + math.tanh(beta_proj * (1.0 - eta_proj))
    bent = jnp.tanh(beta_proj * (density - eta_proj))
    return beta_proj * (1.0 - bent * bent) / norm


def real_basis(size):
    place = np.arange(size)
    rows, waves = [], []
    for k in range(size // 2 + 1):
        angle = 2.0 * np.pi * ((k * place) % size) / size
        edge = k == 0 or 2 * k == size
        rows.append(np.cos(angle) * math.sqrt((1.0 if edge else 2.0) / size))
        waves.append(k)
        if not edge:
            rows.append(np.sin(angle) * math.sqrt(2.0 / size))
            waves.append(k)
    return np.array(rows), np.array(waves)


def mm(left, right):
    return jnp.dot(left, right, precision=highest, preferred_element_type=jnp.float32)


def strip_of(tile, up):
    low_half = lax.broadcasted_iota(jnp.int32, (8, 128), 0) < HALF
    a, b = tile[:, :128], tile[:, 128:]
    if up:
        return jnp.where(low_half, pltpu.roll(a, HALF, 0), b)
    return jnp.where(low_half, a, pltpu.roll(b, HALF, 0))


def split(x):
    high = x.astype(jnp.bfloat16).astype(jnp.float32)
    return high, x - high


def mix(table, x, start=0):
    total = table[start] * x[:1]
    for k in range(1, x.shape[0]):
        total = total + table[start + k] * x[k : k + 1]
    return total


def placed(x, at, size):
    rows = x.shape[0]
    block = lax.broadcasted_iota(jnp.int32, (size, x.shape[1]), 0) // rows
    return jnp.where(block == at, jnp.concatenate([x] * (size // rows)), 0.0)


def transform(x, basis):
    rows, columns = x.shape
    parts = jnp.concatenate(split(x)).astype(jnp.bfloat16)
    product = jnp.dot(parts, basis[...].astype(jnp.bfloat16), preferred_element_type=jnp.float32)
    small = product[rows:, :columns] + product[:rows, columns:] + product[rows:, columns:]
    return product[:rows, :columns] + small


def unpack(strips, st, scale_ref, layers, planes, eps, rows_own, gy):
    rows = rows_own + 2 * HALF
    low_half = lax.broadcasted_iota(jnp.int32, (8, 128), 0) < HALF
    low_half_at = jnp.where(low_half, 0, 1)
    for l in layers:
        for c in range(planes):
            if strips.shape[0] == 2:
                lo, hi = strips[0, c, l], strips[1, c, l]
                left = jnp.where(low_half, hi, pltpu.roll(lo, HALF, 0))
                right = jnp.where(low_half, pltpu.roll(hi, HALF, 0), lo)
            else:
                v = strips[0, c, l]
                w = pltpu.roll(v, HALF, 0)
                keep = low_half_at == gy
                left = jnp.where(keep, jnp.where(low_half, v, w), 0.0)
                right = jnp.where(keep, jnp.where(low_half, w, v), 0.0)
            tile = jnp.concatenate([left, right], axis=1)
            if c == 12:
                scale_ref[l, rows_own:rows, :] = courant * tile
                scale_ref[l, :rows_own, :] = courant * eps[l]
            else:
                st[c, l, rows_own:rows, :] = tile


def updates(st, scale_ref, depth, rows_own):
    rows, nx = st.shape[-2:]
    n_z, n_gy = 2 * lax.axis_size("gz"), lax.axis_size("gy")
    gy = lax.axis_index("gy")
    first_layer = (2 * lax.axis_index("gz") + lax.axis_index("col")) * depth
    row_at = lax.broadcasted_iota(jnp.int32, (rows, nx), 0)
    lane_at = lax.broadcasted_iota(jnp.int32, (rows, 128), 1)
    last_lane, first_lane = lane_at == 127, lane_at == 0
    ahead = jnp.where(gy < n_gy - 1, courant, 0.0)
    behind = jnp.where(gy > 0, courant, 0.0)
    coef_in = jnp.where(row_at < rows_own, courant, jnp.where(row_at < rows_own + HALF, ahead, behind))
    low_layer = depth - first_layer
    high_layer = low_layer + depth * n_z

    def y_ahead(f):
        return pltpu.roll(f, rows - 1, 0)

    def y_behind(f):
        return pltpu.roll(f, 1, 0)

    def x_ahead(f):
        a, b = pltpu.roll(f[:, :128], 127, 1), pltpu.roll(f[:, 128:], 127, 1)
        return jnp.concatenate([jnp.where(last_lane, b, a), jnp.where(last_lane, 0.0, b)], axis=1)

    def x_behind(f):
        a, b = pltpu.roll(f[:, :128], 1, 1), pltpu.roll(f[:, 128:], 1, 1)
        return jnp.concatenate([jnp.where(first_lane, 0.0, a), jnp.where(first_lane, a, b)], axis=1)

    def magnetic(z, whole):
        coef = coef_in * jnp.where((z >= low_layer) & (z < high_layer), 1.0, 0.0)
        for b in (0, 6):
            ex, ey, ez = st[b, z], st[b + 1, z], st[b + 2, z]
            ex_n, ey_n = st[b, z + 1], st[b + 1, z + 1]
            st[b + 3, z] = st[b + 3, z] - coef * ((y_ahead(ez) - ez) - (ey_n - ey))
            st[b + 4, z] = st[b + 4, z] - coef * ((ex_n - ex) - (x_ahead(ez) - ez))
            if whole:
                st[b + 5, z] = st[b + 5, z] - coef * ((x_ahead(ey) - ey) - (y_ahead(ex) - ex))

    def electric(z, b):
        scale = scale_ref[z]
        hx_p, hy_p = st[b + 3, z - 1], st[b + 4, z - 1]
        hx, hy, hz = st[b + 3, z], st[b + 4, z], st[b + 5, z]
        ex = st[b, z] + scale * ((hz - y_behind(hz)) - (hy - hy_p))
        ey = st[b + 1, z] + scale * ((hx - hx_p) - (hz - x_behind(hz)))
        ez = st[b + 2, z] + scale * ((hy - x_behind(hy)) - (hx - y_behind(hx)))
        return ex, ey, ez, hx, hy, hz

    def first_step(magnetic_layers, electric_layers):
        for z in magnetic_layers:
            magnetic(z, z >= 1)
        for z in electric_layers:
            for b in (0, 6):
                for c, f in enumerate(electric(z, b)[:3]):
                    st[b + c, z] = f

    return magnetic, electric, first_step


def early_kernel(cfg, *refs):
    depth, rows_own, sides, second = cfg
    it = iter(refs)
    take = lambda n: [next(it) for _ in range(n)]
    full = take(2)
    strip_in = [take(2) for _ in range(sides)]
    if second:
        (scale_ref, st, strips, sem_full, sem_strip) = take(5)
        eps = eps_in = None
    else:
        (eps_sib, st, scale_ref, strips, eps, sem_full, sem_strip, sem_eps) = take(8)
        eps_in = [full[0].at[12], eps_sib]
    gy, core = lax.axis_index("gy"), lax.axis_index("col")
    planes = 12 if second else 13

    def run(places, base):
        copies = []
        for b, place in enumerate(places):
            layers = pl.ds(place * depth, depth)
            copies.append(
                pltpu.make_async_copy(
                    full[b].at[pl.ds(0, 12)], st.at[:, layers, pl.ds(0, rows_own), :], sem_full.at[b]
                )
            )
            for s in range(sides):
                copies.append(pltpu.make_async_copy(strip_in[s][b], strips.at[s, :, layers], sem_strip.at[s, b]))
            if not second:
                copies.append(pltpu.make_async_copy(eps_in[b], eps.at[layers], sem_eps.at[b]))
        for copy in copies:
            copy.start()
        for copy in copies:
            copy.wait()
        unpack(strips, st, scale_ref, range(base, base + 2 * depth), planes, eps, rows_own, gy)
        first_step = updates(st, scale_ref, depth, rows_own)[2]
        first_step(range(base, base + 2 * depth - 1), range(base + 1, base + 2 * depth - 1))

    @pl.when(core == 0)
    def _():
        run((1, 2), depth)

    @pl.when(core != 0)
    def _():
        run((1, 0), 0)


def window_kernel(cfg, *refs):
    depth, rows_own, sides, second = cfg
    it = iter(refs)
    take = lambda n: [next(it) for _ in range(n)]
    n_z, n_gy = 2 * lax.axis_size("gz"), lax.axis_size("gy")
    core, gy = lax.axis_index("col"), lax.axis_index("gy")
    first_layer = (2 * lax.axis_index("gz") + core) * depth
    layer_start = depth * n_z // 2 - depth - depth // 2
    near = take(2 if second else 1)
    strip_in = take(sides)
    take(1)
    (scale_ref,) = take(1)
    if second:
        (acc_in,) = take(1)
        row_wide, col_table, slope, basis_x, basis_xt, basis_y, basis_yt, response = take(8)
        st, out, share = take(3)
        strips, acc, done, sem_full, sem_strip, sem_out = take(6)
    else:
        st, scale_ref = take(2)
        done = take(3)
        (acc,) = take(1)
        strip_out = take(sides)
        strips, eps, sem_full, sem_strip, sem_eps = take(5)
    nx = st.shape[-1]
    n_layers = 3 * depth
    magnetic, electric, first_step = updates(st, scale_ref, depth, rows_own)

    def start(place):
        layers = pl.ds(place * depth, depth)
        copies = []
        for p, ref in enumerate(near):
            count = min(ref.shape[0], 12)
            copies.append(
                pltpu.make_async_copy(
                    ref.at[pl.ds(0, count)],
                    st.at[pl.ds(count * p, count), layers, pl.ds(0, rows_own), :],
                    sem_full.at[p],
                )
            )
        for s in range(sides):
            copies.append(pltpu.make_async_copy(strip_in[s], strips.at[s, :, layers], sem_strip.at[s]))
        if not second:
            copies.append(pltpu.make_async_copy(near[0].at[12], eps.at[layers], sem_eps))
        for copy in copies:
            copy.start()
        for copy in copies:
            copy.wait()
        layers = range(place * depth, (place + 1) * depth)
        unpack(strips, st, scale_ref, layers, 12 if second else 13, None if second else eps, rows_own, gy)

    @pl.when(core == 0)
    def _():
        start(0)
        first_step(range(depth), range(1, depth + 1))

    @pl.when(core != 0)
    def _():
        start(2)
        layers = range(2 * depth - 1, n_layers - 1)
        first_step(layers, layers)

    angle = omega_step * (1 + (HALF if second else 0))
    w_re, w_im = math.cos(angle), math.sin(angle)
    for own in range(depth):
        for k in range(6):
            e = st[6 * (k // 3) + k % 3, depth + own, :rows_own, :]
            if second:
                acc[0, k, own] = acc_in[0, k, own] + e * w_re
                acc[1, k, own] = acc_in[1, k, own] - e * w_im
            else:
                acc[0, k, own] = e * w_re
                acc[1, k, own] = -(e * w_im)

    column_sum = jnp.zeros((rows_own, nx), jnp.float32)
    for m in range(2, HALF + 1):
        angle = omega_step * (m + (HALF if second else 0))
        w_re, w_im = math.cos(angle), math.sin(angle)
        for z in range(m - 1, n_layers - m):
            magnetic(z, z >= m)
        for z in range(m, n_layers - m):
            own = z - depth
            last = []
            for r in range(2):
                b = 6 * r
                now = electric(z, b)
                for c, f in enumerate(now):
                    if m < HALF:
                        if c < 3:
                            st[b + c, z] = f
                        continue
                    if second:
                        done[b + c, own] = f[:rows_own]
                    else:
                        done[r][c, own] = f[:rows_own]
                        done[2][b + c, own] = f[:rows_own]
                        up, down = f[rows_own - 8 : rows_own], f[:8]
                        if sides == 2:
                            strip_out[0][b + c, own] = strip_of(up, True)
                            strip_out[1][b + c, own] = strip_of(down, False)
                        else:
                            strip_out[0][b + c, own] = jnp.where(gy == 0, strip_of(up, True), strip_of(down, False))
                if 0 <= own < depth:
                    for c, e in enumerate(now[:3]):
                        e = e[:rows_own]
                        re = acc[0, 3 * r + c, own] + e * w_re
                        im = acc[1, 3 * r + c, own] - e * w_im
                        if second and m == HALF:
                            last += [re, im]
                        else:
                            acc[0, 3 * r + c, own], acc[1, 3 * r + c, own] = re, im
            if last:
                g = jnp.zeros((rows_own, nx), jnp.float32)
                for c in range(3):
                    g = g + last[2 * c] * last[2 * c + 6] - last[2 * c + 1] * last[2 * c + 7]
                layer = first_layer + own - layer_start
                column_sum = column_sum + jnp.where((layer >= 0) & (layer < 3 * depth), g, 0.0)

    if second:
        result = pltpu.make_async_copy(done, out, sem_out)
        result.start()
        pooled = jnp.zeros(row_wide.shape[1:], jnp.float32)
        for k in range(rows_own):
            pooled = pooled + row_wide[k] * column_sum[k : k + 1]
        high, rest = split(pooled)
        mid, low = split(rest)
        parts = jnp.concatenate([high, mid, low, jnp.zeros_like(low)]).astype(jnp.bfloat16)
        parts = jnp.dot(parts, col_table[...].astype(jnp.bfloat16), preferred_element_type=jnp.float32)
        band = pooled.shape[0]
        sens = (parts[:band] + parts[band : 2 * band] + parts[2 * band : 3 * band]) * (eps_span / (STEPS * 3 * depth))
        weighted = sens * slope[...]
        tall = response.shape[0]
        if len(basis_y.shape) == 3:
            spectrum = transform(mix(basis_yt, weighted, gy * band), basis_xt) * response[...]
            shares = mix(basis_y, transform(spectrum, basis_x))
        else:
            spectrum = transform(mm(basis_y[...], placed(weighted, gy, tall)), basis_xt) * response[...]
            shares = mm(basis_yt[...], transform(spectrum, basis_x))
        count = share.shape[0]
        for d in range(count):
            y = d // 2 % n_gy
            share[d] = shares[y * band : (y + 1) * band]
        result.wait()


def table_kernel(row_counts, col_counts, row_wide, col_table):
    band, nx = row_wide.shape[1:]
    row = lax.broadcasted_iota(jnp.int32, (band, nx), 0)
    start = jnp.zeros((band, nx), jnp.int32)
    stop = jnp.zeros((band, nx), jnp.int32)
    total = jnp.int32(0)
    for k in range(band):
        start = jnp.where(row == k, total, start)
        total = total + row_counts[0, k]
        stop = jnp.where(row == k, total, stop)
    for p in range(row_wide.shape[0]):
        row_wide[p] = jnp.where((start <= p) & (p < stop), 1.0, 0.0)
    width = col_table.shape[1]
    counts = jnp.broadcast_to(col_counts[...].astype(jnp.float32), (16, width))
    before = lax.broadcasted_iota(jnp.int32, (width, width), 0) <= lax.broadcasted_iota(jnp.int32, (width, width), 1)
    upto = jnp.where(before, 1.0, 0.0).astype(jnp.bfloat16)
    ends = jnp.dot(counts.astype(jnp.bfloat16), upto, preferred_element_type=jnp.float32)
    starts = ends - counts
    place = lax.broadcasted_iota(jnp.int32, col_table.shape, 0).astype(jnp.float32)
    col_table[...] = jnp.where((place >= starts[:1]) & (place < ends[:1]), 1.0, 0.0)


def body(fields, eps_inv, row_counts, col_counts, density):
    runs, comps, depth, rows_own, nx = fields.shape
    n_gz, n_gy = lax.axis_size("gz"), lax.axis_size("gy")
    gz, gy, core = lax.axis_index("gz"), lax.axis_index("gy"), lax.axis_index("col")
    index = gz * 2 + core
    n_z = n_gz * 2
    assert HALF == depth and rows_own == 16 and nx == 256
    rows = rows_own + 2 * HALF
    own = jnp.concatenate([fields.reshape(runs * comps, depth, rows_own, nx), eps_inv[None]])
    own = lax.optimization_barrier(own)

    def swap_core(x):
        return lax.ppermute(x, "col", [(0, 1), (1, 0)])

    def cross(x):
        pairs = []
        for c in range(n_gz - 1):
            a, b = 2 * c + 1, 2 * c + 2
            pairs += [(a, b), (b, a)]
        return lax.ppermute(x, Z, pairs)

    if n_gy == 2:
        ways = [{0: 1, 1: 0}]
    else:
        ways = [{y: y + 1 for y in range(n_gy - 1)}, {y: y - 1 for y in range(1, n_gy)}]
    sides = len(ways)

    def along_y(x, s):
        return lax.ppermute(x, "gy", list(ways[s].items()))

    anywhere = pl.BlockSpec(memory_space=pl.ANY)
    vmem = pl.BlockSpec(memory_space=pltpu.VMEM)
    smem = pl.BlockSpec(memory_space=pltpu.SMEM)
    shape = lambda *s: jax.ShapeDtypeStruct(s, jnp.float32)
    limit = pltpu.CompilerParams(vmem_limit_bytes=24 * 1024 * 1024)

    def strips_sent(strips):
        sent = []
        for s, strip in enumerate(strips):
            mine = along_y(strip, s)
            far = cross(mine)
            sent += [far, mine, swap_core(mine)]
        return sent

    def here(sent):
        return [strip for at, strip in enumerate(sent) if at % 3]

    starts = [(1 - gy) * (rows_own - HALF)] if sides == 1 else [rows_own - HALF, 0]
    strips = []
    for start in starts:
        edge = lax.dynamic_slice_in_dim(own, start, HALF, 2)
        strips.append(jnp.concatenate([edge[..., :128], edge[..., 128:]], 2))
    sent = strips_sent(strips)
    near = cross(own)
    cost = pl.CostEstimate(flops=20_000_000, bytes_accessed=4_000_000, transcendentals=0)
    wide = (12, 3 * depth, rows, nx)
    sems = pltpu.SemaphoreType.DMA
    sibling = swap_core(fields.reshape(runs * comps, depth, rows_own, nx))
    window, scale = pl.pallas_call(
        functools.partial(early_kernel, (depth, rows_own, sides, False)),
        out_shape=(shape(*wide), shape(3 * depth, rows, nx)),
        in_specs=[anywhere] * (3 + 2 * sides),
        out_specs=(vmem, vmem),
        scratch_shapes=[
            pltpu.VMEM((sides, 13, 3 * depth, 8, 128), jnp.float32),
            pltpu.VMEM((3 * depth, rows_own, nx), jnp.float32),
            sems((2,)),
            sems((sides, 2)),
            sems((2,)),
        ],
        compiler_params=limit,
        cost_estimate=cost,
    )(own, sibling, *here(sent), swap_core(eps_inv))
    window, scale, half_0, half_1, state, acc, *strips = pl.pallas_call(
        functools.partial(window_kernel, (depth, rows_own, sides, False)),
        out_shape=(
            shape(*wide),
            shape(3 * depth, rows, nx),
            shape(comps, depth, rows_own, nx),
            shape(comps, depth, rows_own, nx),
            shape(runs * comps, depth, rows_own, nx),
            shape(2, 6, depth, rows_own, nx),
        )
        + (shape(12, depth, 8, 128),) * sides,
        in_specs=[anywhere] * (1 + sides) + [vmem] * 2,
        out_specs=(vmem,) * (6 + sides),
        input_output_aliases={1 + sides: 0, 2 + sides: 1},
        scratch_shapes=[
            pltpu.VMEM((sides, 13, 3 * depth, 8, 128), jnp.float32),
            pltpu.VMEM((3 * depth, rows_own, nx), jnp.float32),
            sems((2,)),
            sems((sides,)),
            sems,
        ],
        compiler_params=limit,
        cost_estimate=cost,
    )(near, *sent[::3], window, scale)

    band, design_cols = density.shape
    tall = band * n_gy
    row_wide, col_table = pl.pallas_call(
        table_kernel,
        out_shape=(shape(rows_own, band, nx), shape(nx, design_cols)),
        in_specs=[smem, vmem],
        out_specs=(vmem, vmem),
        compiler_params=pltpu.CompilerParams(vmem_limit_bytes=4 * 1024 * 1024),
    )(row_counts, col_counts.reshape(1, design_cols))
    basis_x, wave_x = real_basis(design_cols)
    basis_y, wave_y = real_basis(tall)
    response = 1.0 / (
        1.0
        + FILTER_LEN**2
        * (
            4.0 * np.sin(math.pi * wave_y / tall)[:, None] ** 2
            + 4.0 * np.sin(math.pi * wave_x / design_cols)[None, :] ** 2
        )
    )
    const = lambda a: jnp.asarray(a, jnp.float32)
    tables = [basis_y, basis_y.T]
    if tall <= 16:
        tables = [np.broadcast_to(t[:, :, None], (tall, tall, design_cols)) for t in tables]

    def halves(matrix):
        high = matrix.astype(jnp.bfloat16).astype(np.float64)
        return const(np.concatenate([high, matrix - high], axis=1))

    sent = strips_sent(strips)
    window = pl.pallas_call(
        functools.partial(early_kernel, (depth, rows_own, sides, True)),
        out_shape=shape(*wide),
        in_specs=[anywhere] * (2 + 2 * sides) + [vmem],
        out_specs=vmem,
        scratch_shapes=[
            pltpu.VMEM((sides, 12, 3 * depth, 8, 128), jnp.float32),
            sems((2,)),
            sems((sides, 2)),
        ],
        compiler_params=limit,
        cost_estimate=cost,
    )(state, swap_core(state), *here(sent), scale)
    operands = [cross(half_0), cross(half_1), *sent[::3], window, scale, acc]
    operands += [row_wide, col_table, slope_of(density), halves(basis_x), halves(basis_x.T)]
    operands += [const(tables[0]), const(tables[1]), const(response)]
    n_all = n_z * n_gy
    _, fields_out, share = pl.pallas_call(
        functools.partial(window_kernel, (depth, rows_own, sides, True)),
        out_shape=(
            shape(*wide),
            shape(runs * comps, depth, rows_own, nx),
            shape(n_all, band, design_cols),
        ),
        in_specs=[anywhere] * (2 + sides) + [vmem] * 11,
        out_specs=(vmem, anywhere, vmem),
        input_output_aliases={2 + sides: 0},
        scratch_shapes=[
            pltpu.VMEM((sides, 12, 3 * depth, 8, 128), jnp.float32),
            pltpu.VMEM((2, 6, depth, rows_own, nx), jnp.float32),
            pltpu.VMEM((12, depth, rows_own, nx), jnp.float32),
            sems((2,)),
            sems((sides,)),
            sems,
        ],
        compiler_params=limit,
        cost_estimate=cost,
    )(*operands)

    got = lax.all_to_all(share, ("gz", "gy", "col"), 0, 0)
    width = design_cols // n_z
    gradient = lax.dynamic_slice_in_dim(jnp.sum(got, axis=0), index * width, width, 1)
    return fields_out.reshape(fields.shape), gradient


def solution(mesh):
    in_specs = (
        P("groups", None, ("gz", "col"), "gy", None),
        P(("groups", "gz", "col"), "gy", None),
        P(("groups", "gy"), None),
        P("groups"),
        P(("groups", "gy"), None),
    )
    out_specs = (P("groups", None, ("gz", "col"), "gy", None), P(("groups", "gy"), ("gz", "col")))
    return jax.shard_map(body, mesh=mesh, in_specs=in_specs, out_specs=out_specs, check_vma=False)
```

```python
import functools
import math

import jax
import jax.numpy as jnp
import numpy as np
from jax import lax
from jax.experimental import pallas as pl
from jax.experimental.pallas import tpu as pltpu
from jax.sharding import PartitionSpec as P

STEPS = 8
FILTER_LEN = 12

courant = 0.5
omega_step = 0.7
beta_proj = 4.0
eta_proj = 0.5
eps_span = 11.1
highest = lax.Precision.HIGHEST

Z = ("gz", "col")
HALF = STEPS // 2


def slope_of(density):
    norm = math.tanh(beta_proj * eta_proj) + math.tanh(beta_proj * (1.0 - eta_proj))
    bent = jnp.tanh(beta_proj * (density - eta_proj))
    return beta_proj * (1.0 - bent * bent) / norm


def real_basis(size):
    place = np.arange(size)
    rows, waves = [], []
    for k in range(size // 2 + 1):
        angle = 2.0 * np.pi * ((k * place) % size) / size
        edge = k == 0 or 2 * k == size
        rows.append(np.cos(angle) * math.sqrt((1.0 if edge else 2.0) / size))
        waves.append(k)
        if not edge:
            rows.append(np.sin(angle) * math.sqrt(2.0 / size))
            waves.append(k)
    return np.array(rows), np.array(waves)


def mm(left, right):
    return jnp.dot(left, right, precision=highest, preferred_element_type=jnp.float32)


def strip_of(tile, up):
    low_half = lax.broadcasted_iota(jnp.int32, (8, 128), 0) < HALF
    a, b = tile[:, :128], tile[:, 128:]
    if up:
        return jnp.where(low_half, pltpu.roll(a, HALF, 0), b)
    return jnp.where(low_half, a, pltpu.roll(b, HALF, 0))


def split(x):
    high = x.astype(jnp.bfloat16).astype(jnp.float32)
    return high, x - high


def mix(table, x, start=0):
    total = table[start] * x[:1]
    for k in range(1, x.shape[0]):
        total = total + table[start + k] * x[k : k + 1]
    return total


def placed(x, at, size):
    rows = x.shape[0]
    block = lax.broadcasted_iota(jnp.int32, (size, x.shape[1]), 0) // rows
    return jnp.where(block == at, jnp.concatenate([x] * (size // rows)), 0.0)


def transform(x, basis):
    rows, columns = x.shape
    parts = jnp.concatenate(split(x)).astype(jnp.bfloat16)
    product = jnp.dot(parts, basis[...].astype(jnp.bfloat16), preferred_element_type=jnp.float32)
    small = product[rows:, :columns] + product[:rows, columns:] + product[rows:, columns:]
    return product[:rows, :columns] + small


def unpack(strips, st, scale_ref, layers, planes, eps, rows_own, gy):
    rows = rows_own + 2 * HALF
    low_half = lax.broadcasted_iota(jnp.int32, (8, 128), 0) < HALF
    low_half_at = jnp.where(low_half, 0, 1)
    for l in layers:
        for c in range(planes):
            if strips.shape[0] == 2:
                lo, hi = strips[0, c, l], strips[1, c, l]
                left = jnp.where(low_half, hi, pltpu.roll(lo, HALF, 0))
                right = jnp.where(low_half, pltpu.roll(hi, HALF, 0), lo)
            else:
                v = strips[0, c, l]
                w = pltpu.roll(v, HALF, 0)
                keep = low_half_at == gy
                left = jnp.where(keep, jnp.where(low_half, v, w), 0.0)
                right = jnp.where(keep, jnp.where(low_half, w, v), 0.0)
            tile = jnp.concatenate([left, right], axis=1)
            if c == 12:
                scale_ref[l, rows_own:rows, :] = courant * tile
                scale_ref[l, :rows_own, :] = courant * eps[l]
            else:
                st[c, l, rows_own:rows, :] = tile


def updates(st, scale_ref, depth, rows_own):
    rows, nx = st.shape[-2:]
    n_z, n_gy = 2 * lax.axis_size("gz"), lax.axis_size("gy")
    gy = lax.axis_index("gy")
    first_layer = (2 * lax.axis_index("gz") + lax.axis_index("col")) * depth
    row_at = lax.broadcasted_iota(jnp.int32, (rows, nx), 0)
    lane_at = lax.broadcasted_iota(jnp.int32, (rows, 128), 1)
    last_lane, first_lane = lane_at == 127, lane_at == 0
    ahead = jnp.where(gy < n_gy - 1, courant, 0.0)
    behind = jnp.where(gy > 0, courant, 0.0)
    coef_in = jnp.where(row_at < rows_own, courant, jnp.where(row_at < rows_own + HALF, ahead, behind))
    low_layer = depth - first_layer
    high_layer = low_layer + depth * n_z

    def y_ahead(f):
        return pltpu.roll(f, rows - 1, 0)

    def y_behind(f):
        return pltpu.roll(f, 1, 0)

    def x_ahead(f):
        a, b = pltpu.roll(f[:, :128], 127, 1), pltpu.roll(f[:, 128:], 127, 1)
        return jnp.concatenate([jnp.where(last_lane, b, a), jnp.where(last_lane, 0.0, b)], axis=1)

    def x_behind(f):
        a, b = pltpu.roll(f[:, :128], 1, 1), pltpu.roll(f[:, 128:], 1, 1)
        return jnp.concatenate([jnp.where(first_lane, 0.0, a), jnp.where(first_lane, a, b)], axis=1)

    def magnetic(z, whole):
        coef = coef_in * jnp.where((z >= low_layer) & (z < high_layer), 1.0, 0.0)
        for b in (0, 6):
            ex, ey, ez = st[b, z], st[b + 1, z], st[b + 2, z]
            ex_n, ey_n = st[b, z + 1], st[b + 1, z + 1]
            st[b + 3, z] = st[b + 3, z] - coef * ((y_ahead(ez) - ez) - (ey_n - ey))
            st[b + 4, z] = st[b + 4, z] - coef * ((ex_n - ex) - (x_ahead(ez) - ez))
            if whole:
                st[b + 5, z] = st[b + 5, z] - coef * ((x_ahead(ey) - ey) - (y_ahead(ex) - ex))

    def electric(z, b):
        scale = scale_ref[z]
        hx_p, hy_p = st[b + 3, z - 1], st[b + 4, z - 1]
        hx, hy, hz = st[b + 3, z], st[b + 4, z], st[b + 5, z]
        ex = st[b, z] + scale * ((hz - y_behind(hz)) - (hy - hy_p))
        ey = st[b + 1, z] + scale * ((hx - hx_p) - (hz - x_behind(hz)))
        ez = st[b + 2, z] + scale * ((hy - x_behind(hy)) - (hx - y_behind(hx)))
        return ex, ey, ez, hx, hy, hz

    def step(m, magnetic_layers, electric_layers, acc, second):
        for z in magnetic_layers:
            magnetic(z, z >= m)
        angle = omega_step * (m + (HALF if second else 0))
        w_re, w_im = math.cos(angle), math.sin(angle)
        for z in electric_layers:
            own = z - depth
            for r in range(2):
                for c, e in enumerate(electric(z, 6 * r)[:3]):
                    st[6 * r + c, z] = e
                    if not 0 <= own < depth:
                        continue
                    k = 3 * r + c
                    re, im = e[:rows_own] * w_re, e[:rows_own] * w_im
                    if m == 1 and not second:
                        acc[0, k, own], acc[1, k, own] = re, -im
                    else:
                        acc[0, k, own] = acc[0, k, own] + re
                        acc[1, k, own] = acc[1, k, own] - im

    return magnetic, electric, step


def early_kernel(cfg, *refs):
    depth, rows_own, sides, second = cfg
    it = iter(refs)
    take = lambda n: [next(it) for _ in range(n)]
    full = take(2)
    strip_in = [take(2) for _ in range(sides)]
    if second:
        (scale_ref, _, st, acc, strips, sem_full, sem_strip) = take(7)
        eps = eps_in = None
    else:
        (eps_sib, st, scale_ref, acc, strips, eps, sem_full, sem_strip, sem_eps) = take(9)
        eps_in = [full[0].at[12], eps_sib]
    gy, core = lax.axis_index("gy"), lax.axis_index("col")
    planes = 12 if second else 13

    def run(places, base):
        copies = []
        for b, place in enumerate(places):
            layers = pl.ds(place * depth, depth)
            copies.append(
                pltpu.make_async_copy(
                    full[b].at[pl.ds(0, 12)], st.at[:, layers, pl.ds(0, rows_own), :], sem_full.at[b]
                )
            )
            for s in range(sides):
                copies.append(pltpu.make_async_copy(strip_in[s][b], strips.at[s, :, layers], sem_strip.at[s, b]))
            if not second:
                copies.append(pltpu.make_async_copy(eps_in[b], eps.at[layers], sem_eps.at[b]))
        for copy in copies:
            copy.start()
        for copy in copies:
            copy.wait()
        unpack(strips, st, scale_ref, range(base, base + 2 * depth), planes, eps, rows_own, gy)
        step = updates(st, scale_ref, depth, rows_own)[2]
        for m in range(1, HALF):
            top = base + 2 * depth - m
            step(m, range(base + m - 1, top), range(base + m, top), acc, second)

    @pl.when(core == 0)
    def _():
        run((1, 2), depth)

    @pl.when(core != 0)
    def _():
        run((1, 0), 0)


def window_kernel(cfg, *refs):
    depth, rows_own, sides, second = cfg
    it = iter(refs)
    take = lambda n: [next(it) for _ in range(n)]
    n_z, n_gy = 2 * lax.axis_size("gz"), lax.axis_size("gy")
    core, gy = lax.axis_index("col"), lax.axis_index("gy")
    first_layer = (2 * lax.axis_index("gz") + core) * depth
    layer_start = depth * n_z // 2 - depth - depth // 2
    near = take(2 if second else 1)
    strip_in = take(sides)
    take(1)
    scale_ref, _ = take(2)
    if second:
        row_wide, col_table, slope, basis_x, basis_xt, basis_y, basis_yt, response = take(8)
        st, acc, out, share = take(4)
        strips, done, sem_full, sem_strip, sem_out = take(5)
    else:
        st, scale_ref = take(2)
        done = take(3)
        (acc,) = take(1)
        strip_out = take(sides)
        strips, eps, sem_full, sem_strip, sem_eps = take(5)
    nx = st.shape[-1]
    n_layers = 3 * depth
    magnetic, electric, step = updates(st, scale_ref, depth, rows_own)

    def start(place):
        layers = pl.ds(place * depth, depth)
        copies = []
        for p, ref in enumerate(near):
            count = min(ref.shape[0], 12)
            copies.append(
                pltpu.make_async_copy(
                    ref.at[pl.ds(0, count)],
                    st.at[pl.ds(count * p, count), layers, pl.ds(0, rows_own), :],
                    sem_full.at[p],
                )
            )
        for s in range(sides):
            copies.append(pltpu.make_async_copy(strip_in[s], strips.at[s, :, layers], sem_strip.at[s]))
        if not second:
            copies.append(pltpu.make_async_copy(near[0].at[12], eps.at[layers], sem_eps))
        for copy in copies:
            copy.start()
        for copy in copies:
            copy.wait()
        layers = range(place * depth, (place + 1) * depth)
        unpack(strips, st, scale_ref, layers, 12 if second else 13, None if second else eps, rows_own, gy)

    @pl.when(core == 0)
    def _():
        start(0)
        for m in range(1, HALF):
            step(m, range(m - 1, m + depth - 1), range(m, m + depth), acc, second)

    @pl.when(core != 0)
    def _():
        start(2)
        for m in range(1, HALF):
            layers = range(2 * depth - m, n_layers - m)
            step(m, layers, layers, acc, second)

    column_sum = jnp.zeros((rows_own, nx), jnp.float32)
    for m in range(HALF, HALF + 1):
        angle = omega_step * (m + (HALF if second else 0))
        w_re, w_im = math.cos(angle), math.sin(angle)
        for z in range(m - 1, n_layers - m):
            magnetic(z, z >= m)
        for z in range(m, n_layers - m):
            own = z - depth
            last = []
            for r in range(2):
                b = 6 * r
                now = electric(z, b)
                for c, f in enumerate(now):
                    if m < HALF:
                        if c < 3:
                            st[b + c, z] = f
                        continue
                    if second:
                        done[b + c, own] = f[:rows_own]
                    else:
                        done[r][c, own] = f[:rows_own]
                        done[2][b + c, own] = f[:rows_own]
                        up, down = f[rows_own - 8 : rows_own], f[:8]
                        if sides == 2:
                            strip_out[0][b + c, own] = strip_of(up, True)
                            strip_out[1][b + c, own] = strip_of(down, False)
                        else:
                            strip_out[0][b + c, own] = jnp.where(gy == 0, strip_of(up, True), strip_of(down, False))
                if 0 <= own < depth:
                    for c, e in enumerate(now[:3]):
                        e = e[:rows_own]
                        re = acc[0, 3 * r + c, own] + e * w_re
                        im = acc[1, 3 * r + c, own] - e * w_im
                        if second and m == HALF:
                            last += [re, im]
                        else:
                            acc[0, 3 * r + c, own], acc[1, 3 * r + c, own] = re, im
            if last:
                g = jnp.zeros((rows_own, nx), jnp.float32)
                for c in range(3):
                    g = g + last[2 * c] * last[2 * c + 6] - last[2 * c + 1] * last[2 * c + 7]
                layer = first_layer + own - layer_start
                column_sum = column_sum + jnp.where((layer >= 0) & (layer < 3 * depth), g, 0.0)

    if second:
        result = pltpu.make_async_copy(done, out, sem_out)
        result.start()
        pooled = jnp.zeros(row_wide.shape[1:], jnp.float32)
        for k in range(rows_own):
            pooled = pooled + row_wide[k] * column_sum[k : k + 1]
        high, rest = split(pooled)
        mid, low = split(rest)
        parts = jnp.concatenate([high, mid, low, jnp.zeros_like(low)]).astype(jnp.bfloat16)
        parts = jnp.dot(parts, col_table[...].astype(jnp.bfloat16), preferred_element_type=jnp.float32)
        band = pooled.shape[0]
        sens = (parts[:band] + parts[band : 2 * band] + parts[2 * band : 3 * band]) * (eps_span / (STEPS * 3 * depth))
        weighted = sens * slope[...]
        tall = response.shape[0]
        if len(basis_y.shape) == 3:
            spectrum = transform(mix(basis_yt, weighted, gy * band), basis_xt) * response[...]
            shares = mix(basis_y, transform(spectrum, basis_x))
        else:
            spectrum = transform(mm(basis_y[...], placed(weighted, gy, tall)), basis_xt) * response[...]
            shares = mm(basis_yt[...], transform(spectrum, basis_x))
        count = share.shape[0]
        for d in range(count):
            y = d // 2 % n_gy
            share[d] = shares[y * band : (y + 1) * band]
        result.wait()


def table_kernel(row_counts, col_counts, row_wide, col_table):
    band, nx = row_wide.shape[1:]
    row = lax.broadcasted_iota(jnp.int32, (band, nx), 0)
    start = jnp.zeros((band, nx), jnp.int32)
    stop = jnp.zeros((band, nx), jnp.int32)
    total = jnp.int32(0)
    for k in range(band):
        start = jnp.where(row == k, total, start)
        total = total + row_counts[0, k]
        stop = jnp.where(row == k, total, stop)
    for p in range(row_wide.shape[0]):
        row_wide[p] = jnp.where((start <= p) & (p < stop), 1.0, 0.0)
    width = col_table.shape[1]
    counts = jnp.broadcast_to(col_counts[...].astype(jnp.float32), (16, width))
    before = lax.broadcasted_iota(jnp.int32, (width, width), 0) <= lax.broadcasted_iota(jnp.int32, (width, width), 1)
    upto = jnp.where(before, 1.0, 0.0).astype(jnp.bfloat16)
    ends = jnp.dot(counts.astype(jnp.bfloat16), upto, preferred_element_type=jnp.float32)
    starts = ends - counts
    place = lax.broadcasted_iota(jnp.int32, col_table.shape, 0).astype(jnp.float32)
    col_table[...] = jnp.where((place >= starts[:1]) & (place < ends[:1]), 1.0, 0.0)


def body(fields, eps_inv, row_counts, col_counts, density):
    runs, comps, depth, rows_own, nx = fields.shape
    n_gz, n_gy = lax.axis_size("gz"), lax.axis_size("gy")
    gz, gy, core = lax.axis_index("gz"), lax.axis_index("gy"), lax.axis_index("col")
    index = gz * 2 + core
    n_z = n_gz * 2
    assert HALF == depth and rows_own == 16 and nx == 256
    rows = rows_own + 2 * HALF
    own = jnp.concatenate([fields.reshape(runs * comps, depth, rows_own, nx), eps_inv[None]])
    own = lax.optimization_barrier(own)

    def swap_core(x):
        return lax.ppermute(x, "col", [(0, 1), (1, 0)])

    def cross(x):
        pairs = []
        for c in range(n_gz - 1):
            a, b = 2 * c + 1, 2 * c + 2
            pairs += [(a, b), (b, a)]
        return lax.ppermute(x, Z, pairs)

    if n_gy == 2:
        ways = [{0: 1, 1: 0}]
    else:
        ways = [{y: y + 1 for y in range(n_gy - 1)}, {y: y - 1 for y in range(1, n_gy)}]
    sides = len(ways)

    def along_y(x, s):
        return lax.ppermute(x, "gy", list(ways[s].items()))

    anywhere = pl.BlockSpec(memory_space=pl.ANY)
    vmem = pl.BlockSpec(memory_space=pltpu.VMEM)
    smem = pl.BlockSpec(memory_space=pltpu.SMEM)
    shape = lambda *s: jax.ShapeDtypeStruct(s, jnp.float32)
    limit = pltpu.CompilerParams(vmem_limit_bytes=24 * 1024 * 1024)

    def strips_sent(strips):
        sent = []
        for s, strip in enumerate(strips):
            mine = along_y(strip, s)
            far = cross(mine)
            sent += [far, mine, swap_core(mine)]
        return sent

    def here(sent):
        return [strip for at, strip in enumerate(sent) if at % 3]

    starts = [(1 - gy) * (rows_own - HALF)] if sides == 1 else [rows_own - HALF, 0]
    strips = []
    for start in starts:
        edge = lax.dynamic_slice_in_dim(own, start, HALF, 2)
        strips.append(jnp.concatenate([edge[..., :128], edge[..., 128:]], 2))
    sent = strips_sent(strips)
    near = cross(own)
    cost = pl.CostEstimate(flops=20_000_000, bytes_accessed=4_000_000, transcendentals=0)
    wide = (12, 3 * depth, rows, nx)
    sems = pltpu.SemaphoreType.DMA
    sibling = swap_core(fields.reshape(runs * comps, depth, rows_own, nx))
    window, scale, acc = pl.pallas_call(
        functools.partial(early_kernel, (depth, rows_own, sides, False)),
        out_shape=(shape(*wide), shape(3 * depth, rows, nx), shape(2, 6, depth, rows_own, nx)),
        in_specs=[anywhere] * (3 + 2 * sides),
        out_specs=(vmem, vmem, vmem),
        scratch_shapes=[
            pltpu.VMEM((sides, 13, 3 * depth, 8, 128), jnp.float32),
            pltpu.VMEM((3 * depth, rows_own, nx), jnp.float32),
            sems((2,)),
            sems((sides, 2)),
            sems((2,)),
        ],
        compiler_params=limit,
        cost_estimate=cost,
    )(own, sibling, *here(sent), swap_core(eps_inv))
    window, scale, half_0, half_1, state, acc, *strips = pl.pallas_call(
        functools.partial(window_kernel, (depth, rows_own, sides, False)),
        out_shape=(
            shape(*wide),
            shape(3 * depth, rows, nx),
            shape(comps, depth, rows_own, nx),
            shape(comps, depth, rows_own, nx),
            shape(runs * comps, depth, rows_own, nx),
            shape(2, 6, depth, rows_own, nx),
        )
        + (shape(12, depth, 8, 128),) * sides,
        in_specs=[anywhere] * (1 + sides) + [vmem] * 3,
        out_specs=(vmem,) * (6 + sides),
        input_output_aliases={1 + sides: 0, 2 + sides: 1, 3 + sides: 5},
        scratch_shapes=[
            pltpu.VMEM((sides, 13, 3 * depth, 8, 128), jnp.float32),
            pltpu.VMEM((3 * depth, rows_own, nx), jnp.float32),
            sems((2,)),
            sems((sides,)),
            sems,
        ],
        compiler_params=limit,
        cost_estimate=cost,
    )(near, *sent[::3], window, scale, acc)

    band, design_cols = density.shape
    tall = band * n_gy
    row_wide, col_table = pl.pallas_call(
        table_kernel,
        out_shape=(shape(rows_own, band, nx), shape(nx, design_cols)),
        in_specs=[smem, vmem],
        out_specs=(vmem, vmem),
        compiler_params=pltpu.CompilerParams(vmem_limit_bytes=4 * 1024 * 1024),
    )(row_counts, col_counts.reshape(1, design_cols))
    basis_x, wave_x = real_basis(design_cols)
    basis_y, wave_y = real_basis(tall)
    response = 1.0 / (
        1.0
        + FILTER_LEN**2
        * (
            4.0 * np.sin(math.pi * wave_y / tall)[:, None] ** 2
            + 4.0 * np.sin(math.pi * wave_x / design_cols)[None, :] ** 2
        )
    )
    const = lambda a: jnp.asarray(a, jnp.float32)
    tables = [basis_y, basis_y.T]
    if tall <= 16:
        tables = [np.broadcast_to(t[:, :, None], (tall, tall, design_cols)) for t in tables]

    def halves(matrix):
        high = matrix.astype(jnp.bfloat16).astype(np.float64)
        return const(np.concatenate([high, matrix - high], axis=1))

    sent = strips_sent(strips)
    window, acc = pl.pallas_call(
        functools.partial(early_kernel, (depth, rows_own, sides, True)),
        out_shape=(shape(*wide), shape(2, 6, depth, rows_own, nx)),
        in_specs=[anywhere] * (2 + 2 * sides) + [vmem] * 2,
        out_specs=(vmem, vmem),
        input_output_aliases={3 + 2 * sides: 1},
        scratch_shapes=[
            pltpu.VMEM((sides, 12, 3 * depth, 8, 128), jnp.float32),
            sems((2,)),
            sems((sides, 2)),
        ],
        compiler_params=limit,
        cost_estimate=cost,
    )(state, swap_core(state), *here(sent), scale, acc)
    operands = [cross(half_0), cross(half_1), *sent[::3], window, scale, acc]
    operands += [row_wide, col_table, slope_of(density), halves(basis_x), halves(basis_x.T)]
    operands += [const(tables[0]), const(tables[1]), const(response)]
    n_all = n_z * n_gy
    _, _, fields_out, share = pl.pallas_call(
        functools.partial(window_kernel, (depth, rows_own, sides, True)),
        out_shape=(
            shape(*wide),
            shape(2, 6, depth, rows_own, nx),
            shape(runs * comps, depth, rows_own, nx),
            shape(n_all, band, design_cols),
        ),
        in_specs=[anywhere] * (2 + sides) + [vmem] * 11,
        out_specs=(vmem, vmem, anywhere, vmem),
        input_output_aliases={2 + sides: 0, 4 + sides: 1},
        scratch_shapes=[
            pltpu.VMEM((sides, 12, 3 * depth, 8, 128), jnp.float32),
            pltpu.VMEM((12, depth, rows_own, nx), jnp.float32),
            sems((2,)),
            sems((sides,)),
            sems,
        ],
        compiler_params=limit,
        cost_estimate=cost,
    )(*operands)

    got = lax.all_to_all(share, ("gz", "gy", "col"), 0, 0)
    width = design_cols // n_z
    gradient = lax.dynamic_slice_in_dim(jnp.sum(got, axis=0), index * width, width, 1)
    return fields_out.reshape(fields.shape), gradient


def solution(mesh):
    in_specs = (
        P("groups", None, ("gz", "col"), "gy", None),
        P(("groups", "gz", "col"), "gy", None),
        P(("groups", "gy"), None),
        P("groups"),
        P(("groups", "gy"), None),
    )
    out_specs = (P("groups", None, ("gz", "col"), "gy", None), P(("groups", "gy"), ("gz", "col")))
    return jax.shard_map(body, mesh=mesh, in_specs=in_specs, out_specs=out_specs, check_vma=False)
```

```python
import functools
import math

import jax
import jax.numpy as jnp
import numpy as np
from jax import lax
from jax.experimental import pallas as pl
from jax.experimental.pallas import tpu as pltpu
from jax.sharding import PartitionSpec as P

STEPS = 8
FILTER_LEN = 12

courant = 0.5
omega_step = 0.7
beta_proj = 4.0
eta_proj = 0.5
eps_span = 11.1
highest = lax.Precision.HIGHEST

Z = ("gz", "col")
HALF = STEPS // 2


def slope_of(density):
    norm = math.tanh(beta_proj * eta_proj) + math.tanh(beta_proj * (1.0 - eta_proj))
    bent = jnp.tanh(beta_proj * (density - eta_proj))
    return beta_proj * (1.0 - bent * bent) / norm


def real_basis(size):
    place = np.arange(size)
    rows, waves = [], []
    for k in range(size // 2 + 1):
        angle = 2.0 * np.pi * ((k * place) % size) / size
        edge = k == 0 or 2 * k == size
        rows.append(np.cos(angle) * math.sqrt((1.0 if edge else 2.0) / size))
        waves.append(k)
        if not edge:
            rows.append(np.sin(angle) * math.sqrt(2.0 / size))
            waves.append(k)
    return np.array(rows), np.array(waves)


def mm(left, right):
    return jnp.dot(left, right, precision=highest, preferred_element_type=jnp.float32)


def strip_of(tile, up):
    low_half = lax.broadcasted_iota(jnp.int32, (8, 128), 0) < HALF
    a, b = tile[:, :128], tile[:, 128:]
    if up:
        return jnp.where(low_half, pltpu.roll(a, HALF, 0), b)
    return jnp.where(low_half, a, pltpu.roll(b, HALF, 0))


def split(x):
    high = x.astype(jnp.bfloat16).astype(jnp.float32)
    return high, x - high


def mix(table, x, start=0):
    total = table[start] * x[:1]
    for k in range(1, x.shape[0]):
        total = total + table[start + k] * x[k : k + 1]
    return total


def placed(x, at, size):
    rows = x.shape[0]
    block = lax.broadcasted_iota(jnp.int32, (size, x.shape[1]), 0) // rows
    return jnp.where(block == at, jnp.concatenate([x] * (size // rows)), 0.0)


def transform(x, basis):
    rows, columns = x.shape
    parts = jnp.concatenate(split(x)).astype(jnp.bfloat16)
    product = jnp.dot(parts, basis[...].astype(jnp.bfloat16), preferred_element_type=jnp.float32)
    small = product[rows:, :columns] + product[:rows, columns:] + product[rows:, columns:]
    return product[:rows, :columns] + small


def unpack(strips, st, scale_ref, layers, planes, eps, rows_own, gy):
    rows = rows_own + 2 * HALF
    low_half = lax.broadcasted_iota(jnp.int32, (8, 128), 0) < HALF
    low_half_at = jnp.where(low_half, 0, 1)
    for l in layers:
        for c in range(planes):
            if strips.shape[0] == 2:
                lo, hi = strips[0, c, l], strips[1, c, l]
                left = jnp.where(low_half, hi, pltpu.roll(lo, HALF, 0))
                right = jnp.where(low_half, pltpu.roll(hi, HALF, 0), lo)
            else:
                v = strips[0, c, l]
                w = pltpu.roll(v, HALF, 0)
                keep = low_half_at == gy
                left = jnp.where(keep, jnp.where(low_half, v, w), 0.0)
                right = jnp.where(keep, jnp.where(low_half, w, v), 0.0)
            tile = jnp.concatenate([left, right], axis=1)
            if c == 12:
                scale_ref[l, rows_own:rows, :] = courant * tile
                scale_ref[l, :rows_own, :] = courant * eps[l]
            else:
                st[c, l, rows_own:rows, :] = tile


def updates(st, scale_ref, depth, rows_own):
    rows, nx = st.shape[-2:]
    n_z, n_gy = 2 * lax.axis_size("gz"), lax.axis_size("gy")
    gy = lax.axis_index("gy")
    first_layer = (2 * lax.axis_index("gz") + lax.axis_index("col")) * depth
    row_at = lax.broadcasted_iota(jnp.int32, (rows, nx), 0)
    lane_at = lax.broadcasted_iota(jnp.int32, (rows, 128), 1)
    last_lane, first_lane = lane_at == 127, lane_at == 0
    ahead = jnp.where(gy < n_gy - 1, courant, 0.0)
    behind = jnp.where(gy > 0, courant, 0.0)
    coef_in = jnp.where(row_at < rows_own, courant, jnp.where(row_at < rows_own + HALF, ahead, behind))
    low_layer = depth - first_layer
    high_layer = low_layer + depth * n_z

    def y_ahead(f):
        return pltpu.roll(f, rows - 1, 0)

    def y_behind(f):
        return pltpu.roll(f, 1, 0)

    def x_ahead(f):
        a, b = pltpu.roll(f[:, :128], 127, 1), pltpu.roll(f[:, 128:], 127, 1)
        return jnp.concatenate([jnp.where(last_lane, b, a), jnp.where(last_lane, 0.0, b)], axis=1)

    def x_behind(f):
        a, b = pltpu.roll(f[:, :128], 1, 1), pltpu.roll(f[:, 128:], 1, 1)
        return jnp.concatenate([jnp.where(first_lane, 0.0, a), jnp.where(first_lane, a, b)], axis=1)

    def magnetic(z, whole):
        coef = coef_in * jnp.where((z >= low_layer) & (z < high_layer), 1.0, 0.0)
        for b in (0, 6):
            ex, ey, ez = st[b, z], st[b + 1, z], st[b + 2, z]
            ex_n, ey_n = st[b, z + 1], st[b + 1, z + 1]
            st[b + 3, z] = st[b + 3, z] - coef * ((y_ahead(ez) - ez) - (ey_n - ey))
            st[b + 4, z] = st[b + 4, z] - coef * ((ex_n - ex) - (x_ahead(ez) - ez))
            if whole:
                st[b + 5, z] = st[b + 5, z] - coef * ((x_ahead(ey) - ey) - (y_ahead(ex) - ex))

    def electric(z, b):
        scale = scale_ref[z]
        hx_p, hy_p = st[b + 3, z - 1], st[b + 4, z - 1]
        hx, hy, hz = st[b + 3, z], st[b + 4, z], st[b + 5, z]
        ex = st[b, z] + scale * ((hz - y_behind(hz)) - (hy - hy_p))
        ey = st[b + 1, z] + scale * ((hx - hx_p) - (hz - x_behind(hz)))
        ez = st[b + 2, z] + scale * ((hy - x_behind(hy)) - (hx - y_behind(hx)))
        return ex, ey, ez, hx, hy, hz

    def step(m, magnetic_layers, electric_layers, acc, second):
        for z in magnetic_layers:
            magnetic(z, z >= m)
        angle = omega_step * (m + (HALF if second else 0))
        w_re, w_im = math.cos(angle), math.sin(angle)
        for z in electric_layers:
            own = z - depth
            for r in range(2):
                for c, e in enumerate(electric(z, 6 * r)[:3]):
                    st[6 * r + c, z] = e
                    if not 0 <= own < depth:
                        continue
                    k = 3 * r + c
                    re, im = e[:rows_own] * w_re, e[:rows_own] * w_im
                    if m == 1 and not second:
                        acc[0, k, own], acc[1, k, own] = re, -im
                    else:
                        acc[0, k, own] = acc[0, k, own] + re
                        acc[1, k, own] = acc[1, k, own] - im

    return magnetic, electric, step


def early_kernel(cfg, *refs):
    depth, rows_own, sides, second = cfg
    it = iter(refs)
    take = lambda n: [next(it) for _ in range(n)]
    full = take(2)
    strip_in = [take(2) for _ in range(sides)]
    if second:
        (scale_ref, _, st, acc, strips, sem_full, sem_strip) = take(7)
        eps = eps_in = None
    else:
        (st, scale_ref, acc, strips, eps, sem_full, sem_strip, sem_eps) = take(8)
        eps_in = [full[0].at[12], full[1].at[12]]
    gy, core = lax.axis_index("gy"), lax.axis_index("col")
    planes = 12 if second else 13

    def run(places, base):
        copies = []
        for b, place in enumerate(places):
            layers = pl.ds(place * depth, depth)
            copies.append(
                pltpu.make_async_copy(
                    full[b].at[pl.ds(0, 12)], st.at[:, layers, pl.ds(0, rows_own), :], sem_full.at[b]
                )
            )
            for s in range(sides):
                copies.append(pltpu.make_async_copy(strip_in[s][b], strips.at[s, :, layers], sem_strip.at[s, b]))
            if not second:
                copies.append(pltpu.make_async_copy(eps_in[b], eps.at[layers], sem_eps.at[b]))
        for copy in copies:
            copy.start()
        for copy in copies:
            copy.wait()
        unpack(strips, st, scale_ref, range(base, base + 2 * depth), planes, eps, rows_own, gy)
        step = updates(st, scale_ref, depth, rows_own)[2]
        for m in range(1, HALF):
            top = base + 2 * depth - m
            step(m, range(base + m - 1, top), range(base + m, top), acc, second)

    @pl.when(core == 0)
    def _():
        run((1, 2), depth)

    @pl.when(core != 0)
    def _():
        run((1, 0), 0)


def window_kernel(cfg, *refs):
    depth, rows_own, sides, second = cfg
    it = iter(refs)
    take = lambda n: [next(it) for _ in range(n)]
    n_z, n_gy = 2 * lax.axis_size("gz"), lax.axis_size("gy")
    core, gy = lax.axis_index("col"), lax.axis_index("gy")
    first_layer = (2 * lax.axis_index("gz") + core) * depth
    layer_start = depth * n_z // 2 - depth - depth // 2
    near = take(2 if second else 1)
    strip_in = take(sides)
    take(1)
    scale_ref, _ = take(2)
    if second:
        row_wide, col_table, slope, basis_x, basis_xt, basis_y, basis_yt, response = take(8)
        st, acc, out, share = take(4)
        strips, done, sem_full, sem_strip, sem_out = take(5)
    else:
        st, scale_ref = take(2)
        done = take(3)
        (acc,) = take(1)
        strip_out = take(sides)
        strips, eps, sem_full, sem_strip, sem_eps = take(5)
    nx = st.shape[-1]
    n_layers = 3 * depth
    magnetic, electric, step = updates(st, scale_ref, depth, rows_own)

    def start(place):
        layers = pl.ds(place * depth, depth)
        copies = []
        for p, ref in enumerate(near):
            count = min(ref.shape[0], 12)
            copies.append(
                pltpu.make_async_copy(
                    ref.at[pl.ds(0, count)],
                    st.at[pl.ds(count * p, count), layers, pl.ds(0, rows_own), :],
                    sem_full.at[p],
                )
            )
        for s in range(sides):
            copies.append(pltpu.make_async_copy(strip_in[s], strips.at[s, :, layers], sem_strip.at[s]))
        if not second:
            copies.append(pltpu.make_async_copy(near[0].at[12], eps.at[layers], sem_eps))
        for copy in copies:
            copy.start()
        for copy in copies:
            copy.wait()
        layers = range(place * depth, (place + 1) * depth)
        unpack(strips, st, scale_ref, layers, 12 if second else 13, None if second else eps, rows_own, gy)

    @pl.when(core == 0)
    def _():
        start(0)
        for m in range(1, HALF):
            step(m, range(m - 1, m + depth - 1), range(m, m + depth), acc, second)

    @pl.when(core != 0)
    def _():
        start(2)
        for m in range(1, HALF):
            layers = range(2 * depth - m, n_layers - m)
            step(m, layers, layers, acc, second)

    column_sum = jnp.zeros((rows_own, nx), jnp.float32)
    for m in range(HALF, HALF + 1):
        angle = omega_step * (m + (HALF if second else 0))
        w_re, w_im = math.cos(angle), math.sin(angle)
        for z in range(m - 1, n_layers - m):
            magnetic(z, z >= m)
        for z in range(m, n_layers - m):
            own = z - depth
            last = []
            for r in range(2):
                b = 6 * r
                now = electric(z, b)
                for c, f in enumerate(now):
                    if m < HALF:
                        if c < 3:
                            st[b + c, z] = f
                        continue
                    if second:
                        done[b + c, own] = f[:rows_own]
                    else:
                        done[r][c, own] = f[:rows_own]
                        done[2][b + c, own] = f[:rows_own]
                        up, down = f[rows_own - 8 : rows_own], f[:8]
                        if sides == 2:
                            strip_out[0][b + c, own] = strip_of(up, True)
                            strip_out[1][b + c, own] = strip_of(down, False)
                        else:
                            strip_out[0][b + c, own] = jnp.where(gy == 0, strip_of(up, True), strip_of(down, False))
                if 0 <= own < depth:
                    for c, e in enumerate(now[:3]):
                        e = e[:rows_own]
                        re = acc[0, 3 * r + c, own] + e * w_re
                        im = acc[1, 3 * r + c, own] - e * w_im
                        if second and m == HALF:
                            last += [re, im]
                        else:
                            acc[0, 3 * r + c, own], acc[1, 3 * r + c, own] = re, im
            if last:
                g = jnp.zeros((rows_own, nx), jnp.float32)
                for c in range(3):
                    g = g + last[2 * c] * last[2 * c + 6] - last[2 * c + 1] * last[2 * c + 7]
                layer = first_layer + own - layer_start
                column_sum = column_sum + jnp.where((layer >= 0) & (layer < 3 * depth), g, 0.0)

    if second:
        result = pltpu.make_async_copy(done, out, sem_out)
        result.start()
        pooled = jnp.zeros(row_wide.shape[1:], jnp.float32)
        for k in range(rows_own):
            pooled = pooled + row_wide[k] * column_sum[k : k + 1]
        high, rest = split(pooled)
        mid, low = split(rest)
        parts = jnp.concatenate([high, mid, low, jnp.zeros_like(low)]).astype(jnp.bfloat16)
        parts = jnp.dot(parts, col_table[...].astype(jnp.bfloat16), preferred_element_type=jnp.float32)
        band = pooled.shape[0]
        sens = (parts[:band] + parts[band : 2 * band] + parts[2 * band : 3 * band]) * (eps_span / (STEPS * 3 * depth))
        weighted = sens * slope[...]
        tall = response.shape[0]
        if len(basis_y.shape) == 3:
            spectrum = transform(mix(basis_yt, weighted, gy * band), basis_xt) * response[...]
            shares = mix(basis_y, transform(spectrum, basis_x))
        else:
            spectrum = transform(mm(basis_y[...], placed(weighted, gy, tall)), basis_xt) * response[...]
            shares = mm(basis_yt[...], transform(spectrum, basis_x))
        count = share.shape[0]
        for d in range(count):
            y = d // 2 % n_gy
            share[d] = shares[y * band : (y + 1) * band]
        result.wait()


def table_kernel(row_counts, col_counts, row_wide, col_table):
    band, nx = row_wide.shape[1:]
    row = lax.broadcasted_iota(jnp.int32, (band, nx), 0)
    start = jnp.zeros((band, nx), jnp.int32)
    stop = jnp.zeros((band, nx), jnp.int32)
    total = jnp.int32(0)
    for k in range(band):
        start = jnp.where(row == k, total, start)
        total = total + row_counts[0, k]
        stop = jnp.where(row == k, total, stop)
    for p in range(row_wide.shape[0]):
        row_wide[p] = jnp.where((start <= p) & (p < stop), 1.0, 0.0)
    width = col_table.shape[1]
    counts = jnp.broadcast_to(col_counts[...].astype(jnp.float32), (16, width))
    before = lax.broadcasted_iota(jnp.int32, (width, width), 0) <= lax.broadcasted_iota(jnp.int32, (width, width), 1)
    upto = jnp.where(before, 1.0, 0.0).astype(jnp.bfloat16)
    ends = jnp.dot(counts.astype(jnp.bfloat16), upto, preferred_element_type=jnp.float32)
    starts = ends - counts
    place = lax.broadcasted_iota(jnp.int32, col_table.shape, 0).astype(jnp.float32)
    col_table[...] = jnp.where((place >= starts[:1]) & (place < ends[:1]), 1.0, 0.0)


def body(fields, eps_inv, row_counts, col_counts, density):
    runs, comps, depth, rows_own, nx = fields.shape
    n_gz, n_gy = lax.axis_size("gz"), lax.axis_size("gy")
    gz, gy, core = lax.axis_index("gz"), lax.axis_index("gy"), lax.axis_index("col")
    index = gz * 2 + core
    n_z = n_gz * 2
    assert HALF == depth and rows_own == 16 and nx == 256
    rows = rows_own + 2 * HALF
    own = jnp.concatenate([fields.reshape(runs * comps, depth, rows_own, nx), eps_inv[None]])
    own = lax.optimization_barrier(own)

    def swap_core(x):
        return lax.ppermute(x, "col", [(0, 1), (1, 0)])

    def cross(x):
        pairs = []
        for c in range(n_gz - 1):
            a, b = 2 * c + 1, 2 * c + 2
            pairs += [(a, b), (b, a)]
        return lax.ppermute(x, Z, pairs)

    if n_gy == 2:
        ways = [{0: 1, 1: 0}]
    else:
        ways = [{y: y + 1 for y in range(n_gy - 1)}, {y: y - 1 for y in range(1, n_gy)}]
    sides = len(ways)

    def along_y(x, s):
        return lax.ppermute(x, "gy", list(ways[s].items()))

    anywhere = pl.BlockSpec(memory_space=pl.ANY)
    vmem = pl.BlockSpec(memory_space=pltpu.VMEM)
    smem = pl.BlockSpec(memory_space=pltpu.SMEM)
    shape = lambda *s: jax.ShapeDtypeStruct(s, jnp.float32)
    limit = pltpu.CompilerParams(vmem_limit_bytes=24 * 1024 * 1024)

    def strips_sent(strips):
        sent = []
        for s, strip in enumerate(strips):
            mine = along_y(strip, s)
            far = cross(mine)
            sent += [far, mine, swap_core(mine)]
        return sent

    def here(sent):
        return [strip for at, strip in enumerate(sent) if at % 3]

    starts = [(1 - gy) * (rows_own - HALF)] if sides == 1 else [rows_own - HALF, 0]
    strips = []
    for start in starts:
        edge = lax.dynamic_slice_in_dim(own, start, HALF, 2)
        strips.append(jnp.concatenate([edge[..., :128], edge[..., 128:]], 2))
    sent = strips_sent(strips)
    near = cross(own)
    cost = pl.CostEstimate(flops=20_000_000, bytes_accessed=4_000_000, transcendentals=0)
    wide = (12, 3 * depth, rows, nx)
    sems = pltpu.SemaphoreType.DMA
    sibling = swap_core(own)
    window, scale, acc = pl.pallas_call(
        functools.partial(early_kernel, (depth, rows_own, sides, False)),
        out_shape=(shape(*wide), shape(3 * depth, rows, nx), shape(2, 6, depth, rows_own, nx)),
        in_specs=[anywhere] * (2 + 2 * sides),
        out_specs=(vmem, vmem, vmem),
        scratch_shapes=[
            pltpu.VMEM((sides, 13, 3 * depth, 8, 128), jnp.float32),
            pltpu.VMEM((3 * depth, rows_own, nx), jnp.float32),
            sems((2,)),
            sems((sides, 2)),
            sems((2,)),
        ],
        compiler_params=limit,
        cost_estimate=cost,
    )(own, sibling, *here(sent))
    window, scale, half_0, half_1, state, acc, *strips = pl.pallas_call(
        functools.partial(window_kernel, (depth, rows_own, sides, False)),
        out_shape=(
            shape(*wide),
            shape(3 * depth, rows, nx),
            shape(comps, depth, rows_own, nx),
            shape(comps, depth, rows_own, nx),
            shape(runs * comps, depth, rows_own, nx),
            shape(2, 6, depth, rows_own, nx),
        )
        + (shape(12, depth, 8, 128),) * sides,
        in_specs=[anywhere] * (1 + sides) + [vmem] * 3,
        out_specs=(vmem,) * (6 + sides),
        input_output_aliases={1 + sides: 0, 2 + sides: 1, 3 + sides: 5},
        scratch_shapes=[
            pltpu.VMEM((sides, 13, 3 * depth, 8, 128), jnp.float32),
            pltpu.VMEM((3 * depth, rows_own, nx), jnp.float32),
            sems((2,)),
            sems((sides,)),
            sems,
        ],
        compiler_params=limit,
        cost_estimate=cost,
    )(near, *sent[::3], window, scale, acc)

    band, design_cols = density.shape
    tall = band * n_gy
    row_wide, col_table = pl.pallas_call(
        table_kernel,
        out_shape=(shape(rows_own, band, nx), shape(nx, design_cols)),
        in_specs=[smem, vmem],
        out_specs=(vmem, vmem),
        compiler_params=pltpu.CompilerParams(vmem_limit_bytes=4 * 1024 * 1024),
    )(row_counts, col_counts.reshape(1, design_cols))
    basis_x, wave_x = real_basis(design_cols)
    basis_y, wave_y = real_basis(tall)
    response = 1.0 / (
        1.0
        + FILTER_LEN**2
        * (
            4.0 * np.sin(math.pi * wave_y / tall)[:, None] ** 2
            + 4.0 * np.sin(math.pi * wave_x / design_cols)[None, :] ** 2
        )
    )
    const = lambda a: jnp.asarray(a, jnp.float32)
    tables = [basis_y, basis_y.T]
    if tall <= 16:
        tables = [np.broadcast_to(t[:, :, None], (tall, tall, design_cols)) for t in tables]

    def halves(matrix):
        high = matrix.astype(jnp.bfloat16).astype(np.float64)
        return const(np.concatenate([high, matrix - high], axis=1))

    sent = strips_sent(strips)
    window, acc = pl.pallas_call(
        functools.partial(early_kernel, (depth, rows_own, sides, True)),
        out_shape=(shape(*wide), shape(2, 6, depth, rows_own, nx)),
        in_specs=[anywhere] * (2 + 2 * sides) + [vmem] * 2,
        out_specs=(vmem, vmem),
        input_output_aliases={3 + 2 * sides: 1},
        scratch_shapes=[
            pltpu.VMEM((sides, 12, 3 * depth, 8, 128), jnp.float32),
            sems((2,)),
            sems((sides, 2)),
        ],
        compiler_params=limit,
        cost_estimate=cost,
    )(state, swap_core(state), *here(sent), scale, acc)
    operands = [cross(half_0), cross(half_1), *sent[::3], window, scale, acc]
    operands += [row_wide, col_table, slope_of(density), halves(basis_x), halves(basis_x.T)]
    operands += [const(tables[0]), const(tables[1]), const(response)]
    n_all = n_z * n_gy
    _, _, fields_out, share = pl.pallas_call(
        functools.partial(window_kernel, (depth, rows_own, sides, True)),
        out_shape=(
            shape(*wide),
            shape(2, 6, depth, rows_own, nx),
            shape(runs * comps, depth, rows_own, nx),
            shape(n_all, band, design_cols),
        ),
        in_specs=[anywhere] * (2 + sides) + [vmem] * 11,
        out_specs=(vmem, vmem, anywhere, vmem),
        input_output_aliases={2 + sides: 0, 4 + sides: 1},
        scratch_shapes=[
            pltpu.VMEM((sides, 12, 3 * depth, 8, 128), jnp.float32),
            pltpu.VMEM((12, depth, rows_own, nx), jnp.float32),
            sems((2,)),
            sems((sides,)),
            sems,
        ],
        compiler_params=limit,
        cost_estimate=cost,
    )(*operands)

    got = lax.all_to_all(share, ("gz", "gy", "col"), 0, 0)
    width = design_cols // n_z
    gradient = lax.dynamic_slice_in_dim(jnp.sum(got, axis=0), index * width, width, 1)
    return fields_out.reshape(fields.shape), gradient


def solution(mesh):
    in_specs = (
        P("groups", None, ("gz", "col"), "gy", None),
        P(("groups", "gz", "col"), "gy", None),
        P(("groups", "gy"), None),
        P("groups"),
        P(("groups", "gy"), None),
    )
    out_specs = (P("groups", None, ("gz", "col"), "gy", None), P(("groups", "gy"), ("gz", "col")))
    return jax.shard_map(body, mesh=mesh, in_specs=in_specs, out_specs=out_specs, check_vma=False)
```
